128 devices in a mesh: ta: 16 (over y, x_hi, core), gz: 8 (over z, x_lo).
Axes of the slice: x: 4 (x_hi: 2, x_lo: 2; x = x_hi * 2 + x_lo), y: 4, z: 4, core: 2. Of those that a mesh axis runs over, the one named last changes fastest.
Arguments:
- restricted: float32 [16, 96, 16384], P('gz', None, 'ta'), may hold values from -6 to 6
- mass_terms: float32 [96, 16384], P(None, ('ta', 'gz')), may hold values from 2 to 4
- clover_blocks: bfloat16 [96, 96, 16384], P(None, None, ('ta', 'gz')), may hold values from -0.4375 to 0.4375
- hop_links: bfloat16 [8, 96, 96, 16384], P(None, None, None, ('ta', 'gz')), may hold values from -0.21875 to 0.21875
Outputs:
- solution: float32 [16, 96, 16384], P('gz', None, 'ta')
- residual: float32 [16, 96, 16384], P(None, None, ('ta', 'gz'))
The draws below stay inside these ranges and needn't reach their ends.
All inputs are finite; a program needn't handle non-finite values.
Results may differ from the reference program's by a relative error of at most 0.013.
Values may be sent and summed in bfloat16 or wider, within the bound.
A program may use at most 128 MiB of HBM per device.

```python
import jax
import jax.numpy as jnp
from jax import lax

NC = 96
LX = 4
LY = 4
CT = 2
CZ = 4
ITERS = 4
NRHS = 16
SITES = 16384
N_TA = 16
N_GZ = 8


def block_levels(stream_key, shape, pieces, low, high):
    factor_of = 1.0
    for dim, shards_of in pieces:
        heights = jax.random.uniform(jax.random.fold_in(jax.random.fold_in(stream_key, 6), dim), (shards_of,), jnp.float32, low / len(pieces), high / len(pieces))
        factor_of = factor_of * jnp.repeat(jnp.exp(heights), shape[dim] // shards_of).reshape((-1,) + (1,) * (len(shape) - 1 - dim))
    return factor_of


def bell_draw(rng, extent, width, reach, shards=(), kind=jnp.bfloat16):
    array = width * jax.random.normal(rng, extent, jnp.float32)
    if shards:
        array = array * block_levels(rng, extent, shards, -0.22, 0.18)
    return jnp.clip(array, -reach, reach).astype(kind)


def setup_inputs(seed: int = 0) -> dict:
    arg_keys = jax.random.split(jax.random.key(seed), 5)
    return {
        "restricted": bell_draw(arg_keys[0], (NRHS, NC, SITES), 1.0, 6.0, ((0, 8), (2, 16)), jnp.float32),
        "mass_terms": jnp.clip(2.0 + 2.0 * jax.random.uniform(arg_keys[1], (NC, SITES), jnp.float32) ** block_levels(arg_keys[1], (NC, SITES), ((1, 128),), -0.2, 0.2), 2.0, 4.0),
        "clover_blocks": bell_draw(arg_keys[2], (NC, NC, SITES), (NC * 2) ** -0.5, 0.4375, ((2, 128),)),
        "hop_links": bell_draw(arg_keys[3], (8, NC, NC, SITES), (NC * 8) ** -0.5, 0.21875, ((3, 128),)),
    }


def lattice_view(field):
    count = field.shape[0]
    shaped = field.reshape(count, NC, N_TA, N_GZ, CT, CZ, LX, LY)
    return shaped.transpose(0, 1, 2, 4, 3, 5, 6, 7).reshape(count, NC, N_TA * CT, N_GZ * CZ, LX, LY)

def site_view(lattice):
    count = lattice.shape[0]
    shaped = lattice.reshape(count, NC, N_TA, CT, N_GZ, CZ, LX, LY)
    return shaped.transpose(0, 1, 2, 4, 3, 5, 6, 7).reshape(count, NC, -1)

def block_product(matrices, vectors):
    return jnp.einsum('ijs,rjs->ris', matrices.astype(jnp.float32), vectors.astype(jnp.float32))

def coarse_apply(vectors, mass_terms, clover_blocks, hop_links):
    halved = vectors.astype(jnp.bfloat16)
    result = mass_terms[None] * vectors + block_product(clover_blocks, halved)
    lattice = lattice_view(halved)
    shifted_all = [jnp.roll(lattice, -1, 4), jnp.roll(lattice, 1, 4), jnp.roll(lattice, -1, 5), jnp.roll(lattice, 1, 5), jnp.roll(lattice, -1, 3), jnp.roll(lattice, 1, 3), jnp.roll(lattice, -1, 2), jnp.roll(lattice, 1, 2)]
    for number in range(8):
        result = result + block_product(hop_links[number], site_view(shifted_all[number]))
    return result

def inner(left, right):
    return lax.optimization_barrier(jnp.sum(left * right, axis=(1, 2)))

def reference(restricted, mass_terms, clover_blocks, hop_links):
    solution = jnp.zeros_like(restricted)
    residual = restricted
    images = []
    searches = []
    for number in range(ITERS):
        image = coarse_apply(residual, mass_terms, clover_blocks, hop_links)
        image_out = image
        search = residual
        for earlier in range(number):
            weight = inner(images[earlier], image)[:, None, None]
            image_out = image_out - weight * images[earlier]
            search = search - weight * searches[earlier]
        length = jnp.sqrt(inner(image_out, image_out) + 1e-06)[:, None, None]
        image_out = image_out / length
        search = search / length
        alpha = inner(image_out, residual)[:, None, None]
        solution = solution + alpha * search
        residual = residual - alpha * image_out
        images.append(image_out)
        searches.append(search)
    return (solution, residual)
```

```python
import functools

import jax
import jax.numpy as jnp
from jax import lax
from jax.experimental import pallas as pl
from jax.experimental.pallas import tpu as pltpu
from jax.sharding import PartitionSpec as P

MESH = pl.DeviceIdType.MESH
NC = 96
NRHS = 16
ITERS = 4
LOC = 128
GROUPS = 16
SLOTS = 6
CHUNK = 8
F32 = jnp.float32
BF16 = jnp.bfloat16


def lanes(rows=8):
    return lax.broadcasted_iota(jnp.int32, (rows, 128), 1)


def swap_blocks(xs):
    lane = lanes(xs[0].shape[0])
    for b in (1, 2, 4, 8):
        shift = 8 * b
        high = (lane & shift) != 0
        new = list(xs)
        for r in range(16):
            if r & b == 0:
                low_x, high_x = xs[r], xs[r | b]
                new[r] = jnp.where(high, pltpu.roll(high_x, shift, 1), low_x)
                new[r | b] = jnp.where(high, high_x, pltpu.roll(low_x, 128 - shift, 1))
        xs = new
    return xs


def sum_sites(x):
    lane = lanes(x.shape[0])
    for shift in (1, 2, 4):
        other = jnp.where((lane & shift) == 0, pltpu.roll(x, 128 - shift, 1), pltpu.roll(x, shift, 1))
        x = x + other
    return x


def block_diagonal(first, second):
    rows = first.shape[0]
    zeros = jnp.zeros((128, 128), BF16)
    parts = []
    for k in range(rows // 128):
        span = slice(128 * k, 128 * k + 128)
        parts.append(jnp.concatenate([first[span], zeros], axis=1))
        parts.append(jnp.concatenate([zeros, second[span]], axis=1))
    return jnp.concatenate(parts, axis=0)


def kernel(
    n_ta, n_gz,
    restricted, mass, clover, hops,
    sol_out, res_out,
    links, matrix, perm, stage_in, field_in, ext, shifted, mass_f, res, img, acc,
    part1, part2, back_out, back_in,
    link_sem, in_send, in_recv, halo_send, halo_recv, s1_send, s1_recv, s2_send, s2_recv, out_send, out_recv,
):
    ta = lax.axis_index("ta")
    gz = lax.axis_index("gz")
    per = NRHS // n_gz

    def link_copies(c, slot):
        rows = pl.ds(c * CHUNK, CHUNK)
        copies = [pltpu.make_async_copy(clover.at[rows], links.at[slot, :, 0], link_sem.at[slot, 0])]
        for d in range(8):
            copies.append(
                pltpu.make_async_copy(hops.at[d, rows], links.at[slot, :, d + 1], link_sem.at[slot, d + 1])
            )
        return copies

    for c in range(SLOTS):
        for copy in link_copies(c, c):
            copy.start()

    barrier = pltpu.get_barrier_semaphore()
    for o in range(1, n_gz):
        pl.semaphore_signal(barrier, inc=1, device_id=(ta, (gz + o) % n_gz), device_id_type=MESH)
    for o in range(1, n_ta):
        pl.semaphore_signal(barrier, inc=1, device_id=((ta + o) % n_ta, gz), device_id_type=MESH)

    for b in range(n_gz):
        stage_in[b] = restricted[:, :, 128 * b : 128 * b + 128].astype(BF16)
    rows_i = lax.broadcasted_iota(jnp.int32, (256, 256), 0)
    cols_i = lax.broadcasted_iota(jnp.int32, (256, 256), 1)
    wanted = ((rows_i // 8) % 2) * 128 + (rows_i // 16) * 8 + rows_i % 8
    perm[...] = jnp.where(cols_i == wanted, 1.0, 0.0).astype(BF16)

    pl.semaphore_wait(barrier, n_gz - 1 + n_ta - 1)

    def in_copy(o):
        to = (gz + o) % n_gz
        return pltpu.make_async_remote_copy(
            src_ref=stage_in.at[to],
            dst_ref=field_in.at[pl.ds(gz * per, per)],
            send_sem=in_send.at[o],
            recv_sem=in_recv.at[o],
            device_id=(ta, to),
            device_id_type=MESH,
        )

    for o in range(1, n_gz):
        in_copy(o).start()
    field_in[pl.ds(gz * per, per)] = stage_in[gz]

    def mass_step(c, carry):
        rows = pl.ds(pl.multiple_of(c * 8, 8), 8)
        m = mass[rows, :]
        spread = swap_blocks([m] * 16)
        for g in range(GROUPS):
            mass_f[g, rows, :] = spread[g]
        return carry

    lax.fori_loop(0, NC // 8, mass_step, 0)

    def prepare(c, carry):
        slot = c % SLOTS
        for copy in link_copies(c, slot):
            copy.wait()
        pad = jnp.zeros((32, 128), BF16)
        for pair in range(CHUNK // 2):
            sides = []
            for i2 in range(2):
                block = links[slot, 2 * pair + i2]
                head = block[:5].reshape(5 * NC, 128)
                tail = block[5:].reshape(4 * NC, 128)
                sides.append(jnp.concatenate([head, pad, tail], axis=0))
            both = jnp.concatenate(sides, axis=1)
            turned = lax.dot_general(
                perm[...], both, (((1,), (1,)), ((), ())), preferred_element_type=F32
            ).astype(BF16)
            rows = pl.ds(pl.multiple_of((c * (CHUNK // 2) + pair) * 16, 16), 16)
            for g in range(GROUPS):
                for k in range(7):
                    start = k * 256 + (g % 2) * 128
                    matrix[g // 2, rows, start : start + 128] = turned[
                        16 * g : 16 * g + 16, 128 * k : 128 * k + 128
                    ]

        @pl.when(c + SLOTS < NC // CHUNK)
        def _():
            for copy in link_copies(c + SLOTS, slot):
                copy.start()

        return carry

    def fill(tz, first, second):
        t, z = tz // 4, tz % 4
        lane = lanes(NC)
        low_x = (lane & 4) == 0
        y = lane & 3
        swaps = []
        for half, v in enumerate((first, second)):
            ext[t + 1, z + 1, half] = v.astype(BF16)
            up = jnp.where(y < 3, pltpu.roll(v, 127, 1), pltpu.roll(v, 3, 1))
            down = jnp.where(y > 0, pltpu.roll(v, 1, 1), pltpu.roll(v, 125, 1))
            shifted[2, tz * 2 + half] = up.astype(BF16)
            shifted[3, tz * 2 + half] = down.astype(BF16)
            swaps.append(jnp.where(low_x, pltpu.roll(v, 124, 1), pltpu.roll(v, 4, 1)))
        for half in range(2):
            own, other = swaps[half], swaps[1 - half]
            shifted[0, tz * 2 + half] = jnp.where(low_x, own, other).astype(BF16)
            shifted[1, tz * 2 + half] = jnp.where(low_x, other, own).astype(BF16)

    def halo_copies():
        ta_up, ta_down = (ta + 1) % n_ta, (ta + n_ta - 1) % n_ta
        gz_up, gz_down = (gz + 1) % n_gz, (gz + n_gz - 1) % n_gz
        moves = (
            (ext.at[1, 1:5], ext.at[3, 1:5], (ta_down, gz)),
            (ext.at[2, 1:5], ext.at[0, 1:5], (ta_up, gz)),
            (ext.at[1:3, 1], ext.at[1:3, 5], (ta, gz_down)),
            (ext.at[1:3, 4], ext.at[1:3, 0], (ta, gz_up)),
        )
        return [
            pltpu.make_async_remote_copy(
                src_ref=src, dst_ref=dst, send_sem=halo_send.at[n], recv_sem=halo_recv.at[n],
                device_id=to, device_id_type=MESH,
            )
            for n, (src, dst, to) in enumerate(moves)
        ]

    def near_products(tz, carry):
        t, z = tz // 4, tz % 4
        pad = jnp.zeros((32, 128), BF16)
        sides = []
        for half in range(2):
            g = tz * 2 + half
            pieces = [ext[t + 1, z + 1, half]] + [shifted[d, g] for d in range(4)] + [pad]
            sides.append(jnp.concatenate(pieces, axis=0))
        out = jnp.dot(matrix[tz, :, :1024], block_diagonal(*sides), preferred_element_type=F32)
        acc[tz, 0] = out[:, :128]
        acc[tz, 1] = out[:, 128:]
        return carry

    def far_products(number, tz, carry):
        t, z = tz // 4, tz % 4
        sides = []
        for half in range(2):
            pieces = [
                ext[t + 1, z + 2, half], ext[t + 1, z, half], ext[t + 2, z + 1, half], ext[t, z + 1, half]
            ]
            sides.append(jnp.concatenate(pieces, axis=0))
        out = jnp.dot(matrix[tz, :, 1024:], block_diagonal(*sides), preferred_element_type=F32)
        acc[tz, 0] += out[:, :128]
        acc[tz, 1] += out[:, 128:]
        site = lanes() & 7
        carry = list(carry)
        for half in range(2):
            g = tz * 2 + half
            for ib in range(NC // 8):
                total = acc[tz, half, pl.ds(ib * 64, 8, stride=8), :]
                for s in range(1, 8):
                    total = jnp.where(site == s, acc[tz, half, pl.ds(ib * 64 + s, 8, stride=8), :], total)
                rows = pl.ds(ib * 8, 8)
                r = res[number, g, rows, :]
                q = total + mass_f[g, rows, :] * r
                img[number, g, rows, :] = q
                for j in range(number):
                    carry[j] = carry[j] + img[j, g, rows, :] * q
                carry[number] = carry[number] + q * q
                carry[number + 1] = carry[number + 1] + q * r
        return tuple(carry)

    def total_over_devices(number, value):
        part1[number, gz] = value
        copies = []
        for o in range(1, n_gz):
            copies.append(
                pltpu.make_async_remote_copy(
                    src_ref=part1.at[number, gz], dst_ref=part1.at[number, gz],
                    send_sem=s1_send.at[number, o], recv_sem=s1_recv.at[number, o],
                    device_id=(ta, (gz + o) % n_gz), device_id_type=MESH,
                )
            )
        for copy in copies:
            copy.start()
        for copy in copies:
            copy.wait_recv()
        value = part1[number, 0]
        for o in range(1, n_gz):
            value = value + part1[number, o]
        for copy in copies:
            copy.wait_send()
        part2[number, ta] = value
        copies = []
        for o in range(1, n_ta):
            copies.append(
                pltpu.make_async_remote_copy(
                    src_ref=part2.at[number, ta], dst_ref=part2.at[number, ta],
                    send_sem=s2_send.at[number, o], recv_sem=s2_recv.at[number, o],
                    device_id=((ta + o) % n_ta, gz), device_id_type=MESH,
                )
            )
        for copy in copies:
            copy.start()
        for copy in copies:
            copy.wait_recv()
        value = part2[number, 0]
        for o in range(1, n_ta):
            value = value + part2[number, o]
        for copy in copies:
            copy.wait_send()
        return sum_sites(value)

    lax.fori_loop(0, 4, prepare, 0)
    for o in range(1, n_gz):
        in_copy(o).wait_recv()

    def arrange(c, carry):
        rows = pl.ds(pl.multiple_of(c * 16, 16), 16)
        xs = swap_blocks([field_in[r, rows, :].astype(F32) for r in range(NRHS)])
        for g in range(GROUPS):
            res[0, g, rows, :] = xs[g]
        return carry

    lax.fori_loop(0, NC // 16, arrange, 0)

    def first_fill(tz, carry):
        fill(tz, res[0, tz * 2], res[0, tz * 2 + 1])
        return carry

    lax.fori_loop(0, 8, first_fill, 0)
    for copy in halo_copies():
        copy.start()
    lax.fori_loop(4, NC // CHUNK, prepare, 0)
    for o in range(1, n_gz):
        in_copy(o).wait_send()

    gram = {}
    with_res = []
    coef = []
    sol_coef = []
    for number in range(ITERS):
        if number > 0:
            for copy in halo_copies():
                copy.start()
        lax.fori_loop(0, 8, near_products, 0)
        for copy in halo_copies():
            copy.wait()
        zero = jnp.zeros((8, 128), F32)
        sums = lax.fori_loop(0, 8, functools.partial(far_products, number), (zero,) * (number + 2))
        rows = [jnp.sum(x, axis=0, keepdims=True) for x in sums]
        value = jnp.concatenate(rows + [jnp.zeros((8 - len(rows), 128), F32)], axis=0)
        value = total_over_devices(number, value)
        beta = [value[j : j + 1] for j in range(number)]
        squared = value[number : number + 1]
        along = value[number + 1 : number + 2]
        cross = []
        for j in range(number):
            proj = beta[0] * gram[0, j]
            for l in range(1, number):
                proj = proj + beta[l] * gram[l, j]
            cross.append(proj)
        for j in range(number):
            squared = squared - beta[j] * (2.0 * beta[j] - cross[j])
            along = along - beta[j] * with_res[j]
        squared = jnp.maximum(squared, 0.0)
        inverse = 1.0 / jnp.sqrt(squared + 1e-06)
        alpha = along * inverse
        for j in range(number):
            gram[number, j] = gram[j, number] = (beta[j] - cross[j]) * inverse
        gram[number, number] = squared * inverse * inverse
        with_res = [w - alpha * gram[j, number] for j, w in enumerate(with_res)]
        with_res.append(alpha - alpha * gram[number, number])
        mine = []
        for m in range(number):
            total = beta[m] * coef[m][m]
            for j in range(m + 1, number):
                total = total + beta[j] * coef[j][m]
            mine.append(-total * inverse)
        mine.append(inverse)
        coef.append(mine)
        sol_coef = [c + alpha * mine[m] for m, c in enumerate(sol_coef)] + [alpha * inverse]

        def update(tz, carry):
            fresh = []
            for half in range(2):
                g = tz * 2 + half
                q = img[number, g]
                for j in range(number):
                    q = q - beta[j] * img[j, g]
                q = q * inverse
                if number < ITERS - 1:
                    img[number, g] = q
                r = res[number, g] - alpha * q
                res[number + 1, g] = r
                fresh.append(r)
            if number < ITERS - 1:
                fill(tz, *fresh)
            return carry

        if number < ITERS - 1:
            lax.fori_loop(0, 8, update, 0)

    def finish(c, carry):
        rows = pl.ds(pl.multiple_of(c * 16, 16), 16)
        xs = []
        for g in range(GROUPS):
            x = sol_coef[0] * res[0, g, rows, :]
            for m in range(1, ITERS):
                x = x + sol_coef[m] * res[m, g, rows, :]
            xs.append(x)
        xs = swap_blocks(xs)
        for r in range(NRHS):
            back_out[r, rows, :] = xs[r].astype(BF16)
        return carry

    lax.fori_loop(0, NC // 16, finish, 0)

    def out_copy(o):
        to = (gz + o) % n_gz
        return pltpu.make_async_remote_copy(
            src_ref=back_out.at[pl.ds(to * per, per)],
            dst_ref=back_in.at[gz],
            send_sem=out_send.at[o],
            recv_sem=out_recv.at[o],
            device_id=(ta, to),
            device_id_type=MESH,
        )

    for o in range(1, n_gz):
        out_copy(o).start()
    back_in[gz] = back_out[pl.ds(gz * per, per)]

    def last_residual(c, carry):
        rows = pl.ds(pl.multiple_of(c * 8, 8), 8)
        xs = []
        for g in range(GROUPS):
            q = img[ITERS - 1, g, rows, :]
            for j in range(ITERS - 1):
                q = q - beta[j] * img[j, g, rows, :]
            xs.append(res[ITERS - 1, g, rows, :] - alpha * (q * inverse))
        xs = swap_blocks(xs)
        for r in range(NRHS):
            res_out[r, rows, :] = xs[r]
        return carry

    lax.fori_loop(0, NC // 8, last_residual, 0)
    for o in range(1, n_gz):
        out_copy(o).wait()
    for b in range(n_gz):
        sol_out[:, :, 128 * b : 128 * b + 128] = back_in[b].astype(F32)


def solution(mesh):
    n_ta, n_gz = mesh.shape["ta"], mesh.shape["gz"]
    per = NRHS // n_gz

    def step(restricted, mass_terms, clover_blocks, hop_links):
        vmem = pl.BlockSpec(memory_space=pltpu.VMEM)
        hbm = pl.BlockSpec(memory_space=pl.ANY)
        dma = pltpu.SemaphoreType.DMA
        return pl.pallas_call(
            functools.partial(kernel, n_ta, n_gz),
            out_shape=(
                jax.ShapeDtypeStruct((per, NC, LOC * n_gz), F32),
                jax.ShapeDtypeStruct((NRHS, NC, LOC), F32),
            ),
            in_specs=[vmem, vmem, hbm, hbm],
            out_specs=(vmem, vmem),
            scratch_shapes=[
                pltpu.VMEM((SLOTS, CHUNK, 9, NC, 128), BF16),
                pltpu.VMEM((8, 8 * NC, 7 * 256), BF16),
                pltpu.VMEM((256, 256), BF16),
                pltpu.VMEM((n_gz, per, NC, 128), BF16),
                pltpu.VMEM((NRHS, NC, 128), BF16),
                pltpu.VMEM((4, 6, 2, NC, 128), BF16),
                pltpu.VMEM((4, GROUPS, NC, 128), BF16),
                pltpu.VMEM((GROUPS, NC, 128), F32),
                pltpu.VMEM((ITERS, GROUPS, NC, 128), F32),
                pltpu.VMEM((ITERS, GROUPS, NC, 128), F32),
                pltpu.VMEM((8, 2, 8 * NC, 128), F32),
                pltpu.VMEM((ITERS, n_gz, 8, 128), F32),
                pltpu.VMEM((ITERS, n_ta, 8, 128), F32),
                pltpu.VMEM((NRHS, NC, 128), BF16),
                pltpu.VMEM((n_gz, per, NC, 128), BF16),
                dma((SLOTS, 9)),
                dma((n_gz,)),
                dma((n_gz,)),
                dma((4,)),
                dma((4,)),
                dma((ITERS, n_gz)),
                dma((ITERS, n_gz)),
                dma((ITERS, n_ta)),
                dma((ITERS, n_ta)),
                dma((n_gz,)),
                dma((n_gz,)),
            ],
            compiler_params=pltpu.CompilerParams(
                collective_id=0, has_side_effects=True, vmem_limit_bytes=60 * 1024 * 1024
            ),
        )(restricted, mass_terms, clover_blocks, hop_links)

    return jax.shard_map(
        step,
        mesh=mesh,
        in_specs=(
            P("gz", None, "ta"),
            P(None, ("ta", "gz")),
            P(None, None, ("ta", "gz")),
            P(None, None, None, ("ta", "gz")),
        ),
        out_specs=(P("gz", None, "ta"), P(None, None, ("ta", "gz"))),
        check_vma=False,
    )
```

```python
import functools

import jax
import jax.numpy as jnp
from jax import lax
from jax.experimental import pallas as pl
from jax.experimental.pallas import tpu as pltpu
from jax.sharding import PartitionSpec as P

MESH = pl.DeviceIdType.MESH
NC = 96
NRHS = 16
ITERS = 4
LOC = 128
GROUPS = 16
SLOTS = 6
CHUNK = 8
SHIFT = 3.0
F32 = jnp.float32
BF16 = jnp.bfloat16


def lanes(rows=8):
    return lax.broadcasted_iota(jnp.int32, (rows, 128), 1)


def swap_blocks(xs):
    lane = lanes(xs[0].shape[0])
    for b in (1, 2, 4, 8):
        shift = 8 * b
        high = (lane & shift) != 0
        new = list(xs)
        for r in range(16):
            if r & b == 0:
                low_x, high_x = xs[r], xs[r | b]
                new[r] = jnp.where(high, pltpu.roll(high_x, shift, 1), low_x)
                new[r | b] = jnp.where(high, high_x, pltpu.roll(low_x, 128 - shift, 1))
        xs = new
    return xs


def sum_sites(x):
    lane = lanes(x.shape[0])
    for shift in (1, 2, 4):
        other = jnp.where((lane & shift) == 0, pltpu.roll(x, 128 - shift, 1), pltpu.roll(x, shift, 1))
        x = x + other
    return x


def block_diagonal(first, second):
    rows = first.shape[0]
    zeros = jnp.zeros((128, 128), BF16)
    parts = []
    for k in range(rows // 128):
        span = slice(128 * k, 128 * k + 128)
        parts.append(jnp.concatenate([first[span], zeros], axis=1))
        parts.append(jnp.concatenate([zeros, second[span]], axis=1))
    return jnp.concatenate(parts, axis=0)


def kernel(
    n_ta, n_gz,
    restricted, mass, clover, hops,
    sol_out, res_out,
    links, matrix, perm, stage_in, field_in, own, halo_t, halo_z, ext, mass_f, basis, near, acc,
    part1, part2, back_out, back_in,
    link_sem, in_send, in_recv, t_send, t_recv, z_send, z_recv, s1_send, s1_recv, s2_send, s2_recv, out_send, out_recv,
):
    ta = lax.axis_index("ta")
    gz = lax.axis_index("gz")
    per = NRHS // n_gz
    ta_up, ta_down = (ta + 1) % n_ta, (ta + n_ta - 1) % n_ta
    gz_up, gz_down = (gz + 1) % n_gz, (gz + n_gz - 1) % n_gz
    ta_low, gz_low = min(4, n_ta), min(2, n_gz)
    ta_high, gz_high = n_ta // ta_low, n_gz // gz_low
    th, tl, gh, gl = ta // ta_low, ta % ta_low, gz // gz_low, gz % gz_low
    place1 = tl * gz_low + gl
    place2 = th * gz_high + gh
    peers1 = [
        (th * ta_low + (tl + a) % ta_low, gh * gz_low + (gl + b) % gz_low)
        for a in range(ta_low) for b in range(gz_low) if a or b
    ]
    peers2 = [
        (((th + a) % ta_high) * ta_low + tl, ((gh + b) % gz_high) * gz_low + gl)
        for a in range(ta_high) for b in range(gz_high) if a or b
    ]

    def link_copies(c, slot):
        rows = pl.ds(c * CHUNK, CHUNK)
        copies = [pltpu.make_async_copy(clover.at[rows], links.at[slot, :, 0], link_sem.at[slot, 0])]
        for d in range(8):
            copies.append(
                pltpu.make_async_copy(hops.at[d, rows], links.at[slot, :, d + 1], link_sem.at[slot, d + 1])
            )
        return copies

    barrier = pltpu.get_barrier_semaphore()
    greet = [(ta, (gz + o) % n_gz) for o in range(1, n_gz)] + peers1 + peers2 + [(ta_up, gz), (ta_down, gz)]
    for to in greet:
        pl.semaphore_signal(barrier, inc=1, device_id=to, device_id_type=MESH)

    for c in range(SLOTS):
        for copy in link_copies(c, c):
            copy.start()

    for b in range(n_gz):
        stage_in[b] = restricted[:, :, 128 * b : 128 * b + 128].astype(BF16)
    rows_i = lax.broadcasted_iota(jnp.int32, (256, 256), 0)
    cols_i = lax.broadcasted_iota(jnp.int32, (256, 256), 1)
    wanted = ((rows_i // 8) % 2) * 128 + (rows_i // 16) * 8 + rows_i % 8
    perm[...] = jnp.where(cols_i == wanted, 1.0, 0.0).astype(BF16)

    def mass_step(c, carry):
        rows = pl.ds(pl.multiple_of(c * 16, 16), 16)
        m = mass[rows, :] - SHIFT
        spread = swap_blocks([m] * 16)
        for g in range(GROUPS):
            mass_f[g, rows, :] = spread[g]
        return carry

    lax.fori_loop(0, NC // 16, mass_step, 0, unroll=2)

    pl.semaphore_wait(barrier, len(greet))

    def in_copy(o):
        to = (gz + o) % n_gz
        return pltpu.make_async_remote_copy(
            src_ref=stage_in.at[to],
            dst_ref=field_in.at[pl.ds(gz * per, per)],
            send_sem=in_send.at[o],
            recv_sem=in_recv.at[o],
            device_id=(ta, to),
            device_id_type=MESH,
        )

    for o in range(1, n_gz):
        in_copy(o).start()
    field_in[pl.ds(gz * per, per)] = stage_in[gz]

    def prepare(c, carry):
        slot = c % SLOTS
        for copy in link_copies(c, slot):
            copy.wait()
        pad = jnp.zeros((32, 128), BF16)
        for pair in range(CHUNK // 2):
            sides = []
            for i2 in range(2):
                block = links[slot, 2 * pair + i2]
                front = block[:5].reshape(5 * NC, 128)
                tail = block[5:].reshape(4 * NC, 128)
                sides.append(jnp.concatenate([front, pad, tail], axis=0))
            both = jnp.concatenate(sides, axis=1)
            turned = lax.dot_general(
                perm[...], both, (((1,), (1,)), ((), ())), preferred_element_type=F32
            ).astype(BF16)
            rows = pl.ds(pl.multiple_of((c * (CHUNK // 2) + pair) * 16, 16), 16)
            for g in range(GROUPS):
                for k in range(7):
                    start = k * 256 + (g % 2) * 128
                    matrix[g // 2, rows, start : start + 128] = turned[
                        16 * g : 16 * g + 16, 128 * k : 128 * k + 128
                    ]

        @pl.when(c + SLOTS < NC // CHUNK)
        def _():
            for copy in link_copies(c + SLOTS, slot):
                copy.start()

        return carry

    def t_copy(m, t, z):
        side = 1 - t
        return pltpu.make_async_remote_copy(
            src_ref=own.at[m, t, z], dst_ref=halo_t.at[m, side, z],
            send_sem=t_send.at[m, side, z], recv_sem=t_recv.at[m, side, z],
            device_id=(ta_up if t else ta_down, gz), device_id_type=MESH,
        )

    def z_copy(m, side):
        return pltpu.make_async_remote_copy(
            src_ref=own.at[m, :, 0 if side else 3], dst_ref=halo_z.at[m, side],
            send_sem=z_send.at[m, side], recv_sem=z_recv.at[m, side],
            device_id=(ta, gz_down if side else gz_up), device_id_type=MESH,
        )

    def send_halo(m, z):
        t_copy(m, 0, z).start()
        t_copy(m, 1, z).start()

        @pl.when(z == 0)
        def _():
            z_copy(m, 1).start()

        @pl.when(z == 3)
        def _():
            z_copy(m, 0).start()

    def chosen(t, half):
        site = lanes() & 7
        parts = []
        for ib in range(NC // 8):
            total = acc[t, half, pl.ds(ib * 64, 8, stride=8), :]
            for s in range(1, 8):
                total = jnp.where(site == s, acc[t, half, pl.ds(ib * 64 + s, 8, stride=8), :], total)
            parts.append(total)
        return jnp.concatenate(parts, axis=0)

    def near_products(k, mix, i, carry):
        z = lax.rem(3 * i, 4)
        lane = lanes(NC)
        low_x = (lane & 4) == 0
        y = lane & 3
        pad = jnp.zeros((32, 128), BF16)
        for t in range(2):
            vs, swaps, sides = [], [], []
            for half in range(2):
                g = (t * 4 + z) * 2 + half
                if k < 2:
                    v = basis[k, g]
                else:
                    v = mix[0] * basis[1, g]
                    for m in range(1, k):
                        v = v + mix[m] * basis[m + 1, g]
                vs.append(v)
                swaps.append(jnp.where(low_x, pltpu.roll(v, 124, 1), pltpu.roll(v, 4, 1)))
            for half in range(2):
                v, here, there = vs[half], swaps[half], swaps[1 - half]
                center = v.astype(BF16)
                ext[t + 1, z + 1, half] = center
                pieces = [
                    center,
                    jnp.where(low_x, here, there).astype(BF16),
                    jnp.where(low_x, there, here).astype(BF16),
                    jnp.where(y < 3, pltpu.roll(v, 127, 1), pltpu.roll(v, 3, 1)).astype(BF16),
                    jnp.where(y > 0, pltpu.roll(v, 1, 1), pltpu.roll(v, 125, 1)).astype(BF16),
                    pad,
                ]
                sides.append(jnp.concatenate(pieces, axis=0))
            out = jnp.dot(matrix[t * 4 + z, :, :1024], block_diagonal(*sides), preferred_element_type=F32)
            acc[t, 0] = out[:, :128]
            acc[t, 1] = out[:, 128:]
            for half in range(2):
                g = (t * 4 + z) * 2 + half
                near[g] = chosen(t, half) + mass_f[g] * vs[half]
        return carry

    def far_products(k, mix, i, carry):
        z = lax.rem(3 * i, 4)

        def mixed(ref, *at):
            if k < 2:
                return ref[(k, *at)]
            v = mix[0] * ref[(1, *at)].astype(F32)
            for m in range(1, k):
                v = v + mix[m] * ref[(m + 1, *at)].astype(F32)
            return v.astype(BF16)

        for t in range(2):
            t_copy(k, 1 - t, z).wait_recv()
            for half in range(2):
                ext[3 * t, z + 1, half] = mixed(halo_t, t, z, half)

        for edge, side in ((0, 0), (3, 1)):

            @pl.when(z == edge)
            def _():
                z_copy(k, side).wait_recv()
                for t in range(2):
                    for half in range(2):
                        ext[t + 1, 5 * side, half] = mixed(halo_z, side, t, half)

        carry = list(carry)
        for t in range(2):
            sides = []
            for half in range(2):
                pieces = [
                    ext[t + 1, z + 2, half], ext[t + 1, z, half], ext[t + 2, z + 1, half], ext[t, z + 1, half]
                ]
                sides.append(jnp.concatenate(pieces, axis=0))
            out = jnp.dot(matrix[t * 4 + z, :, 1024:], block_diagonal(*sides), preferred_element_type=F32)
            acc[t, 0] = out[:, :128]
            acc[t, 1] = out[:, 128:]
            for half in range(2):
                g = (t * 4 + z) * 2 + half
                new = near[g] + chosen(t, half)
                basis[k + 1, g] = new
                if k < ITERS - 1:
                    own[k + 1, t, z, half] = new.astype(BF16)
                others = [basis[j, g] for j in range(k + 1)]
                products = [other * new for other in others] + [new * new]
                if k == 0:
                    products.append(others[0] * others[0])
                for j, product in enumerate(products):
                    carry[j] = carry[j] + jnp.sum(product.reshape(NC // 8, 8, 128), axis=0)
        if k < ITERS - 1:
            send_halo(k + 1, z)
        return tuple(carry)

    def share(number, stage):
        buf, place, peers, send, recv = (
            (part1, place1, peers1, s1_send, s1_recv), (part2, place2, peers2, s2_send, s2_recv)
        )[stage]
        return [
            pltpu.make_async_remote_copy(
                src_ref=buf.at[number, place], dst_ref=buf.at[number, place],
                send_sem=send.at[number, n], recv_sem=recv.at[number, n],
                device_id=to, device_id_type=MESH,
            )
            for n, to in enumerate(peers)
        ]

    def sum_start(number, value):
        part1[number, place1] = value
        for copy in share(number, 0):
            copy.start()

    def sum_middle(number):
        for copy in share(number, 0):
            copy.wait_recv()
        value = part1[number, 0]
        for n in range(1, ta_low * gz_low):
            value = value + part1[number, n]
        part2[number, place2] = value
        for copy in share(number, 1):
            copy.start()

    def sum_end(number):
        for copy in share(number, 1):
            copy.wait_recv()
        value = part2[number, 0]
        for n in range(1, ta_high * gz_high):
            value = value + part2[number, n]
        return sum_sites(value)

    lax.fori_loop(0, 6, prepare, 0)
    for o in range(1, n_gz):
        in_copy(o).wait_recv()

    def arrange(c, carry):
        rows = pl.ds(pl.multiple_of(c * 16, 16), 16)
        xs = swap_blocks([field_in[r, rows, :].astype(F32) for r in range(NRHS)])
        for g in range(GROUPS):
            basis[0, g, rows, :] = xs[g]
            own[0, g // 8, (g // 2) % 4, g % 2, rows, :] = xs[g].astype(BF16)
        return carry

    lax.fori_loop(0, NC // 16, arrange, 0, unroll=2)
    for z in range(4):
        t_copy(0, 0, z).start()
        t_copy(0, 1, z).start()
    z_copy(0, 1).start()
    z_copy(0, 0).start()
    lax.fori_loop(6, NC // CHUNK, prepare, 0)

    size = ITERS + 1
    gram = {}

    def unit(m):
        return [1.0 if n == m else None for n in range(size)]

    def add(u, c, w):
        out = []
        for a, b in zip(u, w):
            if b is None:
                out.append(a)
            else:
                out.append(c * b if a is None else a + c * b)
        return out

    def scale(c, w):
        return [None if b is None else c * b for b in w]

    def apply_gram(w):
        out = []
        for m in range(size):
            total = None
            for n in range(size):
                if w[n] is not None and (m, n) in gram:
                    term = w[n] * gram[m, n]
                    total = term if total is None else total + term
            out.append(total)
        return out

    def pair_up(u, gw):
        total = None
        for a, b in zip(u, gw):
            if a is not None and b is not None:
                total = a * b if total is None else total + a * b
        return total

    r, p, x = unit(0), unit(1), [None] * size
    images, searches, image_products = [], [], []
    mix = None

    def iterate(k, r, p, x):
        q = add(p, SHIFT, r)
        gq = apply_gram(q)
        betas = [pair_up(image, gq) for image in images]
        qo, po = q, r
        for beta, image, search in zip(betas, images, searches):
            qo, po = add(qo, -beta, image), add(po, -beta, search)
        gqo = apply_gram(qo)
        inverse = 1.0 / jnp.sqrt(jnp.maximum(pair_up(qo, gqo), 0.0) + 1e-06)
        alpha = pair_up(r, gqo) * inverse
        qo, po = scale(inverse, qo), scale(inverse, po)
        x = add(x, alpha, po)
        if k < ITERS - 1:
            bq = add(unit(k + 2), SHIFT, p)
            for beta, product in zip(betas, image_products):
                bq = add(bq, -beta, product)
            bq = scale(inverse, bq)
            image_products.append(bq)
            p = add(p, -alpha, bq)
        r = add(r, -alpha, qo)
        images.append(qo)
        searches.append(po)
        return r, p, x

    def take_gram(k, value):
        for j in range(k + 2):
            gram[j, k + 1] = gram[k + 1, j] = value[j : j + 1]
        if k == 0:
            gram[0, 0] = value[2:3]
            gram[0, 1] = gram[1, 0] = value[0:1]
            gram[1, 1] = value[1:2]

    for k in range(ITERS):
        lax.fori_loop(0, 4, functools.partial(near_products, k, mix), 0)
        if k > 0:
            sum_middle(k - 1)
        count = k + 2 + (k == 0)
        zero = jnp.zeros((8, 128), F32)
        sums = lax.fori_loop(0, 4, functools.partial(far_products, k, mix), (zero,) * count)
        rows = [jnp.sum(v, axis=0, keepdims=True) for v in sums]
        sum_start(k, jnp.concatenate(rows + [jnp.zeros((8 - count, 128), F32)], axis=0))
        if k > 0:
            take_gram(k - 1, sum_end(k - 1))
            r, p, x = iterate(k - 1, r, p, x)
            mix = p[1 : k + 2]
    sum_middle(ITERS - 1)
    take_gram(ITERS - 1, sum_end(ITERS - 1))
    r, p, x = iterate(ITERS - 1, r, p, x)

    def combine(coefs, g, rows):
        total = None
        for m, c in enumerate(coefs):
            if c is not None:
                term = c * basis[m, g, rows, :]
                total = term if total is None else total + term
        return total

    def finish(c, carry):
        rows = pl.ds(pl.multiple_of(c * 16, 16), 16)
        xs = swap_blocks([combine(x, g, rows) for g in range(GROUPS)])
        for n in range(NRHS):
            back_out[n, rows, :] = xs[n].astype(BF16)
        return carry

    lax.fori_loop(0, NC // 16, finish, 0, unroll=2)

    def out_copy(o):
        to = (gz + o) % n_gz
        return pltpu.make_async_remote_copy(
            src_ref=back_out.at[pl.ds(to * per, per)],
            dst_ref=back_in.at[gz],
            send_sem=out_send.at[o],
            recv_sem=out_recv.at[o],
            device_id=(ta, to),
            device_id_type=MESH,
        )

    for o in range(1, n_gz):
        out_copy(o).start()
    back_in[gz] = back_out[pl.ds(gz * per, per)]

    def last_residual(c, carry):
        rows = pl.ds(pl.multiple_of(c * 16, 16), 16)
        xs = swap_blocks([combine(r, g, rows) for g in range(GROUPS)])
        for n in range(NRHS):
            res_out[n, rows, :] = xs[n]
        return carry

    lax.fori_loop(0, NC // 16, last_residual, 0, unroll=2)

    for o in range(1, n_gz):
        in_copy(o).wait_send()
    for m in range(ITERS):
        for z in range(4):
            t_copy(m, 0, z).wait_send()
            t_copy(m, 1, z).wait_send()
        z_copy(m, 0).wait_send()
        z_copy(m, 1).wait_send()
        for stage in range(2):
            for copy in share(m, stage):
                copy.wait_send()
    for o in range(1, n_gz):
        out_copy(o).wait()
    for b in range(n_gz):
        sol_out[:, :, 128 * b : 128 * b + 128] = back_in[b]


def solution(mesh):
    n_ta, n_gz = mesh.shape["ta"], mesh.shape["gz"]
    per = NRHS // n_gz
    first = min(4, n_ta) * min(2, n_gz)
    second = n_ta * n_gz // first

    def step(restricted, mass_terms, clover_blocks, hop_links):
        vmem = pl.BlockSpec(memory_space=pltpu.VMEM)
        hbm = pl.BlockSpec(memory_space=pl.ANY)
        dma = pltpu.SemaphoreType.DMA
        sol, res = pl.pallas_call(
            functools.partial(kernel, n_ta, n_gz),
            out_shape=(
                jax.ShapeDtypeStruct((per, NC, LOC * n_gz), BF16),
                jax.ShapeDtypeStruct((NRHS, NC, LOC), F32),
            ),
            in_specs=[vmem, vmem, hbm, hbm],
            out_specs=(vmem, vmem),
            scratch_shapes=[
                pltpu.VMEM((SLOTS, CHUNK, 9, NC, 128), BF16),
                pltpu.VMEM((8, 8 * NC, 7 * 256), BF16),
                pltpu.VMEM((256, 256), BF16),
                pltpu.VMEM((n_gz, per, NC, 128), BF16),
                pltpu.VMEM((NRHS, NC, 128), BF16),
                pltpu.VMEM((ITERS, 2, 4, 2, NC, 128), BF16),
                pltpu.VMEM((ITERS, 2, 4, 2, NC, 128), BF16),
                pltpu.VMEM((ITERS, 2, 2, 2, NC, 128), BF16),
                pltpu.VMEM((4, 6, 2, NC, 128), BF16),
                pltpu.VMEM((GROUPS, NC, 128), F32),
                pltpu.VMEM((ITERS + 1, GROUPS, NC, 128), F32),
                pltpu.VMEM((GROUPS, NC, 128), F32),
                pltpu.VMEM((2, 2, 8 * NC, 128), F32),
                pltpu.VMEM((ITERS, first, 8, 128), F32),
                pltpu.VMEM((ITERS, second, 8, 128), F32),
                pltpu.VMEM((NRHS, NC, 128), BF16),
                pltpu.VMEM((n_gz, per, NC, 128), BF16),
                dma((SLOTS, 9)),
                dma((n_gz,)),
                dma((n_gz,)),
                dma((ITERS, 2, 4)),
                dma((ITERS, 2, 4)),
                dma((ITERS, 2)),
                dma((ITERS, 2)),
                dma((ITERS, first)),
                dma((ITERS, first)),
                dma((ITERS, second)),
                dma((ITERS, second)),
                dma((n_gz,)),
                dma((n_gz,)),
            ],
            compiler_params=pltpu.CompilerParams(
                collective_id=0, has_side_effects=True, vmem_limit_bytes=60 * 1024 * 1024
            ),
        )(restricted, mass_terms, clover_blocks, hop_links)
        return sol.astype(F32), res

    return jax.shard_map(
        step,
        mesh=mesh,
        in_specs=(
            P("gz", None, "ta"),
            P(None, ("ta", "gz")),
            P(None, None, ("ta", "gz")),
            P(None, None, None, ("ta", "gz")),
        ),
        out_specs=(P("gz", None, "ta"), P(None, None, ("ta", "gz"))),
        check_vma=False,
    )
```

```python
import functools

import jax
import jax.numpy as jnp
from jax import lax
from jax.experimental import pallas as pl
from jax.experimental.pallas import tpu as pltpu
from jax.sharding import PartitionSpec as P

MESH = pl.DeviceIdType.MESH
NC = 96
NRHS = 16
ITERS = 4
LOC = 128
GROUPS = 16
SLOTS = 6
CHUNK = 8
EARLY = 6
SHIFT = 3.0
F32 = jnp.float32
BF16 = jnp.bfloat16


def lanes(rows=8):
    return lax.broadcasted_iota(jnp.int32, (rows, 128), 1)


def swap_blocks(xs):
    lane = lanes(xs[0].shape[0])
    for b in (1, 2, 4, 8):
        shift = 8 * b
        high = (lane & shift) != 0
        new = list(xs)
        for r in range(16):
            if r & b == 0:
                low_x, high_x = xs[r], xs[r | b]
                new[r] = jnp.where(high, pltpu.roll(high_x, shift, 1), low_x)
                new[r | b] = jnp.where(high, high_x, pltpu.roll(low_x, 128 - shift, 1))
        xs = new
    return xs


def sum_sites(x):
    lane = lanes(x.shape[0])
    for shift in (1, 2, 4):
        other = jnp.where((lane & shift) == 0, pltpu.roll(x, 128 - shift, 1), pltpu.roll(x, shift, 1))
        x = x + other
    return x


def block_diagonal(first, second):
    rows = first.shape[0]
    zeros = jnp.zeros((128, 128), BF16)
    parts = []
    for k in range(rows // 128):
        span = slice(128 * k, 128 * k + 128)
        parts.append(jnp.concatenate([first[span], zeros], axis=1))
        parts.append(jnp.concatenate([zeros, second[span]], axis=1))
    return jnp.concatenate(parts, axis=0)


def kernel(
    n_ta, n_gz,
    restricted, mass_in, clover, hops,
    sol_out, res_out,
    links, matrix, perm, stage_in, field_in, own, halo_t, halo_z, ext, mass_f, basis, near, acc,
    part1, part2, back_out, back_in, rhs, mass, res_buf,
    rhs_sem, mass_sem, res_sem, link_sem, in_send, in_recv, t_send, t_recv, z_send, z_recv, s1_send, s1_recv, s2_send, s2_recv, out_send, out_recv,
):
    ta = lax.axis_index("ta")
    gz = lax.axis_index("gz")
    per = NRHS // n_gz
    ta_up, ta_down = (ta + 1) % n_ta, (ta + n_ta - 1) % n_ta
    gz_up, gz_down = (gz + 1) % n_gz, (gz + n_gz - 1) % n_gz
    ta_low, gz_low = min(4, n_ta), min(2, n_gz)
    ta_high, gz_high = n_ta // ta_low, n_gz // gz_low
    th, tl, gh, gl = ta // ta_low, ta % ta_low, gz // gz_low, gz % gz_low
    place1 = tl * gz_low + gl
    place2 = th * gz_high + gh
    peers1 = [
        (th * ta_low + (tl + a) % ta_low, gh * gz_low + (gl + b) % gz_low)
        for a in range(ta_low) for b in range(gz_low) if a or b
    ]
    peers2 = [
        (((th + a) % ta_high) * ta_low + tl, ((gh + b) % gz_high) * gz_low + gl)
        for a in range(ta_high) for b in range(gz_high) if a or b
    ]

    def link_copies(c, slot):
        rows = pl.ds(c * CHUNK, CHUNK)
        copies = [pltpu.make_async_copy(clover.at[rows], links.at[slot, :, 0], link_sem.at[slot, 0])]
        for d in range(8):
            copies.append(
                pltpu.make_async_copy(hops.at[d, rows], links.at[slot, :, d + 1], link_sem.at[slot, d + 1])
            )
        return copies

    rhs_copy = pltpu.make_async_copy(restricted, rhs, rhs_sem)
    rhs_copy.start()
    mass_copy = pltpu.make_async_copy(mass_in, mass, mass_sem)
    mass_copy.start()
    barrier = pltpu.get_barrier_semaphore()
    greet = [(ta, (gz + o) % n_gz) for o in range(1, n_gz)] + peers1 + peers2 + [(ta_up, gz), (ta_down, gz)]
    for to in greet:
        pl.semaphore_signal(barrier, inc=1, device_id=to, device_id_type=MESH)

    rhs_copy.wait()
    for c in range(SLOTS):
        for copy in link_copies(c, c):
            copy.start()
    for b in range(n_gz):
        stage_in[b] = rhs[:, :, 128 * b : 128 * b + 128].astype(BF16)
    pl.semaphore_wait(barrier, len(greet))

    def in_copy(o):
        to = (gz + o) % n_gz
        return pltpu.make_async_remote_copy(
            src_ref=stage_in.at[to],
            dst_ref=field_in.at[pl.ds(gz * per, per)],
            send_sem=in_send.at[o],
            recv_sem=in_recv.at[o],
            device_id=(ta, to),
            device_id_type=MESH,
        )

    for o in range(1, n_gz):
        in_copy(o).start()
    field_in[pl.ds(gz * per, per)] = stage_in[gz]

    rows_i = lax.broadcasted_iota(jnp.int32, (256, 256), 0)
    cols_i = lax.broadcasted_iota(jnp.int32, (256, 256), 1)
    wanted = ((rows_i // 8) % 2) * 128 + (rows_i // 16) * 8 + rows_i % 8
    perm[...] = jnp.where(cols_i == wanted, 1.0, 0.0).astype(BF16)

    def mass_step(c, carry):
        rows = pl.ds(pl.multiple_of(c * 16, 16), 16)
        m = mass[rows, :] - SHIFT
        spread = swap_blocks([m] * 16)
        for g in range(GROUPS):
            mass_f[g, rows, :] = spread[g]
        return carry

    mass_copy.wait()
    lax.fori_loop(0, NC // 16, mass_step, 0, unroll=2)

    def prepare(c, carry):
        slot = c % SLOTS
        for copy in link_copies(c, slot):
            copy.wait()
        pad = jnp.zeros((32, 128), BF16)
        for pair in range(CHUNK // 2):
            sides = []
            for i2 in range(2):
                block = links[slot, 2 * pair + i2]
                front = block[:5].reshape(5 * NC, 128)
                tail = block[5:].reshape(4 * NC, 128)
                sides.append(jnp.concatenate([front, pad, tail], axis=0))
            both = jnp.concatenate(sides, axis=1)
            turned = lax.dot_general(
                perm[...], both, (((1,), (1,)), ((), ())), preferred_element_type=F32
            ).astype(BF16)
            rows = pl.ds(pl.multiple_of((c * (CHUNK // 2) + pair) * 16, 16), 16)
            for g in range(GROUPS):
                for k in range(7):
                    start = k * 256 + (g % 2) * 128
                    matrix[g // 2, rows, start : start + 128] = turned[
                        16 * g : 16 * g + 16, 128 * k : 128 * k + 128
                    ]

        @pl.when(c + SLOTS < NC // CHUNK)
        def _():
            for copy in link_copies(c + SLOTS, slot):
                copy.start()

        return carry

    def t_copy(m, t, z):
        side = 1 - t
        return pltpu.make_async_remote_copy(
            src_ref=own.at[m, t, z], dst_ref=halo_t.at[m, side, z],
            send_sem=t_send.at[m, side, z], recv_sem=t_recv.at[m, side, z],
            device_id=(ta_up if t else ta_down, gz), device_id_type=MESH,
        )

    def z_copy(m, side):
        return pltpu.make_async_remote_copy(
            src_ref=own.at[m, :, 0 if side else 3], dst_ref=halo_z.at[m, side],
            send_sem=z_send.at[m, side], recv_sem=z_recv.at[m, side],
            device_id=(ta, gz_down if side else gz_up), device_id_type=MESH,
        )

    def send_rest(m, z):
        t_copy(m, 1, z).start()

        @pl.when(z == 0)
        def _():
            z_copy(m, 1).start()

        @pl.when(z == 3)
        def _():
            z_copy(m, 0).start()

    def chosen(t, half):
        site = lanes() & 7
        parts = []
        for ib in range(NC // 8):
            total = acc[t, half, pl.ds(ib * 64, 8, stride=8), :]
            for s in range(1, 8):
                total = jnp.where(site == s, acc[t, half, pl.ds(ib * 64 + s, 8, stride=8), :], total)
            parts.append(total)
        return jnp.concatenate(parts, axis=0)

    def z_at(i):
        return lax.rem(3 * i, 4)

    def near_dot(k, mix, t, z):
        lane = lanes(NC)

        def packed(condition):
            return jnp.where(condition, 1.0, 0.0).astype(BF16) > 0.5

        low_x, not_last, not_first = packed((lane & 4) == 0), packed((lane & 3) < 3), packed((lane & 3) > 0)
        pad = jnp.zeros((32, 128), BF16)
        vs, swaps, sides = [], [], []
        for half in range(2):
            g = (t * 4 + z) * 2 + half
            if k < ITERS - 1:
                v = basis[k, g]
            else:
                v = mix[0] * basis[1, g]
                for m in range(1, k):
                    v = v + mix[m] * basis[m + 1, g]
            near[g] = mass_f[g] * v
            v = v.astype(BF16)
            vs.append(v)
            swaps.append(jnp.where(low_x, pltpu.roll(v, 124, 1), pltpu.roll(v, 4, 1)))
        for half in range(2):
            v, here, there = vs[half], swaps[half], swaps[1 - half]
            ext[t + 1, z + 1, half] = v
            pieces = [
                v,
                jnp.where(low_x, here, there),
                jnp.where(low_x, there, here),
                jnp.where(not_last, pltpu.roll(v, 127, 1), pltpu.roll(v, 3, 1)),
                jnp.where(not_first, pltpu.roll(v, 1, 1), pltpu.roll(v, 125, 1)),
                pad,
            ]
            sides.append(jnp.concatenate(pieces, axis=0))
        out = jnp.dot(matrix[t * 4 + z, :, :1024], block_diagonal(*sides), preferred_element_type=F32)
        acc[t, 0] = out[:, :128]
        acc[t, 1] = out[:, 128:]

    def near_take(t, z):
        for half in range(2):
            g = (t * 4 + z) * 2 + half
            near[g] += chosen(t, half)

    def near_products(k, mix, i, carry):
        near_dot(k, mix, 0, z_at(i))
        near_take(1, z_at(i + 3))
        near_dot(k, mix, 1, z_at(i))
        near_take(0, z_at(i))
        return carry

    def far_dot(t, z):
        sides = []
        for half in range(2):
            pieces = [
                ext[t + 1, z + 2, half], ext[t + 1, z, half], ext[t + 2, z + 1, half], ext[t, z + 1, half]
            ]
            sides.append(jnp.concatenate(pieces, axis=0))
        out = jnp.dot(matrix[t * 4 + z, :, 1024:], block_diagonal(*sides), preferred_element_type=F32)
        acc[t, 0] = out[:, :128]
        acc[t, 1] = out[:, 128:]

    def far_take(k, t, z):
        sums = None
        for half in range(2):
            g = (t * 4 + z) * 2 + half
            new = near[g] + chosen(t, half)
            basis[k + 1, g] = new
            if k < ITERS - 1:
                own[k + 1, t, z, half] = new.astype(BF16)
            others = [basis[j, g] for j in range(k + 1)]
            products = [other * new for other in others] + [new * new]
            if k == 0:
                products.append(others[0] * others[0])
            part = [jnp.sum(product.reshape(NC // 8, 8, 128), axis=0) for product in products]
            sums = part if sums is None else [a + b for a, b in zip(sums, part)]
        return sums

    def far_products(k, mix, i, carry):
        z = z_at(i)

        def mixed(ref, *at):
            if k < ITERS - 1:
                return ref[(k, *at)]
            v = mix[0] * ref[(1, *at)].astype(F32)
            for m in range(1, k):
                v = v + mix[m] * ref[(m + 1, *at)].astype(F32)
            return v.astype(BF16)

        for t in range(2):
            t_copy(k, 1 - t, z).wait_recv()
            for half in range(2):
                ext[3 * t, z + 1, half] = mixed(halo_t, t, z, half)

        for edge, side in ((0, 0), (3, 1)):

            @pl.when(z == edge)
            def _():
                z_copy(k, side).wait_recv()
                for t in range(2):
                    for half in range(2):
                        ext[t + 1, 5 * side, half] = mixed(halo_z, side, t, half)

        if k == 2:

            @pl.when(i == 1)
            def _():
                sum_middle(0)

        far_dot(0, z)
        before = far_take(k, 1, z_at(i + 3))
        far_dot(1, z)
        now = far_take(k, 0, z)
        if k < ITERS - 1:
            t_copy(k + 1, 0, z).start()

            @pl.when(i > 0)
            def _():
                send_rest(k + 1, z_at(i + 3))

        return tuple(c + jnp.where(i > 0, b, 0.0) + n for c, b, n in zip(carry, before, now))

    def share(number, stage):
        buf, place, peers, send, recv = (
            (part1, place1, peers1, s1_send, s1_recv), (part2, place2, peers2, s2_send, s2_recv)
        )[stage]
        return [
            pltpu.make_async_remote_copy(
                src_ref=buf.at[number, place], dst_ref=buf.at[number, place],
                send_sem=send.at[number, n], recv_sem=recv.at[number, n],
                device_id=to, device_id_type=MESH,
            )
            for n, to in enumerate(peers)
        ]

    def sum_start(number, value):
        part1[number, place1] = value
        for copy in share(number, 0):
            copy.start()

    def sum_middle(number):
        for copy in share(number, 0):
            copy.wait_recv()
        value = part1[number, 0]
        for n in range(1, ta_low * gz_low):
            value = value + part1[number, n]
        part2[number, place2] = value
        for copy in share(number, 1):
            copy.start()

    def sum_end(number):
        for copy in share(number, 1):
            copy.wait_recv()
        value = part2[number, 0]
        for n in range(1, ta_high * gz_high):
            value = value + part2[number, n]
        return sum_sites(value)

    lax.fori_loop(0, EARLY, prepare, 0)
    for o in range(1, n_gz):
        in_copy(o).wait_recv()

    def arrange(c, carry):
        rows = pl.ds(pl.multiple_of(c * 16, 16), 16)
        xs = swap_blocks([field_in[r, rows, :].astype(F32) for r in range(NRHS)])
        for g in range(GROUPS):
            basis[0, g, rows, :] = xs[g]
            own[0, g // 8, (g // 2) % 4, g % 2, rows, :] = xs[g].astype(BF16)
        return carry

    lax.fori_loop(0, NC // 16, arrange, 0, unroll=2)
    for z in range(4):
        t_copy(0, 0, z).start()
        t_copy(0, 1, z).start()
    z_copy(0, 1).start()
    z_copy(0, 0).start()
    lax.fori_loop(EARLY, NC // CHUNK, prepare, 0)

    size = ITERS + 1
    gram = {}

    def unit(m):
        return [1.0 if n == m else None for n in range(size)]

    def add(u, c, w):
        out = []
        for a, b in zip(u, w):
            if b is None:
                out.append(a)
            else:
                out.append(c * b if a is None else a + c * b)
        return out

    def scale(c, w):
        return [None if b is None else c * b for b in w]

    def apply_gram(w):
        out = []
        for m in range(size):
            total = None
            for n in range(size):
                if w[n] is not None and (m, n) in gram:
                    term = w[n] * gram[m, n]
                    total = term if total is None else total + term
            out.append(total)
        return out

    def pair_up(u, gw):
        total = None
        for a, b in zip(u, gw):
            if a is not None and b is not None:
                total = a * b if total is None else total + a * b
        return total

    r, p, x = unit(0), unit(1), [None] * size
    images, searches, image_products = [], [], []
    mix = None

    def iterate(k, r, p, x):
        q = add(p, SHIFT, r)
        gq = apply_gram(q)
        betas = [pair_up(image, gq) for image in images]
        qo, po = q, r
        for beta, image, search in zip(betas, images, searches):
            qo, po = add(qo, -beta, image), add(po, -beta, search)
        gqo = apply_gram(qo)
        inverse = 1.0 / jnp.sqrt(jnp.maximum(pair_up(qo, gqo), 0.0) + 1e-06)
        alpha = pair_up(r, gqo) * inverse
        qo, po = scale(inverse, qo), scale(inverse, po)
        x = add(x, alpha, po)
        if k < ITERS - 1:
            product = [None] + p[:-1] if k == 1 else unit(k + 2)
            bq = add(product, SHIFT, p)
            for beta, earlier in zip(betas, image_products):
                bq = add(bq, -beta, earlier)
            bq = scale(inverse, bq)
            image_products.append(bq)
            p = add(p, -alpha, bq)
        r = add(r, -alpha, qo)
        images.append(qo)
        searches.append(po)
        return r, p, x

    def take_gram(pairs, value):
        for n, (i, j) in enumerate(pairs):
            gram[i, j] = gram[j, i] = value[n : n + 1]

    pairs, rows = [], []
    for k in range(ITERS):
        lax.fori_loop(0, 4, functools.partial(near_products, k, mix), 0)
        near_take(1, z_at(3))
        new_pairs = [(j, k + 1) for j in range(k + 2)] + ([(0, 0)] if k == 0 else [])
        zero = jnp.zeros((8, 128), F32)
        sums = lax.fori_loop(0, 4, functools.partial(far_products, k, mix), (zero,) * len(new_pairs))
        sums = [a + b for a, b in zip(sums, far_take(k, 1, z_at(3)))]
        pairs += new_pairs
        rows += [jnp.sum(v, axis=0, keepdims=True) for v in sums]
        if k % 2:
            sum_start(k // 2, jnp.concatenate(rows + [jnp.zeros((16 - len(rows), 128), F32)], axis=0))
            sent, pairs, rows = pairs, [], []
        if k < ITERS - 1:
            t_copy(k + 1, 1, z_at(3)).start()
        if k == 2:
            take_gram(sent, sum_end(0))
            for n in range(2):
                r, p, x = iterate(n, r, p, x)
            mix = p[1:4]
    sum_middle(1)
    take_gram(sent, sum_end(1))
    for n in range(2, ITERS):
        r, p, x = iterate(n, r, p, x)

    def combine(coefs, g, rows):
        total = None
        for m, c in enumerate(coefs):
            if c is not None:
                term = c * basis[m, g, rows, :]
                total = term if total is None else total + term
        return total

    def finish(c, carry):
        rows = pl.ds(pl.multiple_of(c * 16, 16), 16)
        xs = swap_blocks([combine(x, g, rows) for g in range(GROUPS)])
        for n in range(NRHS):
            back_out[n, rows, :] = xs[n].astype(BF16)
        return carry

    lax.fori_loop(0, NC // 16, finish, 0, unroll=2)

    def out_copy(o):
        to = (gz + o) % n_gz
        return pltpu.make_async_remote_copy(
            src_ref=back_out.at[pl.ds(to * per, per)],
            dst_ref=back_in.at[gz],
            send_sem=out_send.at[o],
            recv_sem=out_recv.at[o],
            device_id=(ta, to),
            device_id_type=MESH,
        )

    for o in range(1, n_gz):
        out_copy(o).start()
    back_in[gz] = back_out[pl.ds(gz * per, per)]

    def last_residual(c, carry):
        rows = pl.ds(pl.multiple_of(c * 16, 16), 16)
        xs = swap_blocks([combine(r, g, rows) for g in range(GROUPS)])
        for n in range(NRHS):
            res_buf[n, rows, :] = xs[n]
        return carry

    lax.fori_loop(0, NC // 16, last_residual, 0, unroll=2)
    res_copy = pltpu.make_async_copy(res_buf, res_out, res_sem)
    res_copy.start()

    for o in range(1, n_gz):
        in_copy(o).wait_send()
    for m in range(ITERS):
        for z in range(4):
            t_copy(m, 0, z).wait_send()
            t_copy(m, 1, z).wait_send()
        z_copy(m, 0).wait_send()
        z_copy(m, 1).wait_send()
    for number in range(2):
        for stage in range(2):
            for copy in share(number, stage):
                copy.wait_send()
    for o in range(1, n_gz):
        out_copy(o).wait()
    for b in range(n_gz):
        sol_out[:, :, 128 * b : 128 * b + 128] = back_in[b]
    res_copy.wait()


def deliver(sol, res, sol_out, res_out):
    sol_out[...] = sol[...].astype(F32)
    res_out[...] = res[...]


def solution(mesh):
    n_ta, n_gz = mesh.shape["ta"], mesh.shape["gz"]
    per = NRHS // n_gz
    first = min(4, n_ta) * min(2, n_gz)
    second = n_ta * n_gz // first

    def step(restricted, mass_terms, clover_blocks, hop_links):
        vmem = pl.BlockSpec(memory_space=pltpu.VMEM)
        hbm = pl.BlockSpec(memory_space=pl.ANY)
        dma = pltpu.SemaphoreType.DMA
        sol, res = pl.pallas_call(
            functools.partial(kernel, n_ta, n_gz),
            out_shape=(
                jax.ShapeDtypeStruct((per, NC, LOC * n_gz), BF16),
                jax.ShapeDtypeStruct((NRHS, NC, LOC), F32),
            ),
            in_specs=[hbm] * 4,
            out_specs=(vmem, hbm),
            scratch_shapes=[
                pltpu.VMEM((SLOTS, CHUNK, 9, NC, 128), BF16),
                pltpu.VMEM((8, 8 * NC, 7 * 256), BF16),
                pltpu.VMEM((256, 256), BF16),
                pltpu.VMEM((n_gz, per, NC, 128), BF16),
                pltpu.VMEM((NRHS, NC, 128), BF16),
                pltpu.VMEM((ITERS, 2, 4, 2, NC, 128), BF16),
                pltpu.VMEM((ITERS, 2, 4, 2, NC, 128), BF16),
                pltpu.VMEM((ITERS, 2, 2, 2, NC, 128), BF16),
                pltpu.VMEM((4, 6, 2, NC, 128), BF16),
                pltpu.VMEM((GROUPS, NC, 128), F32),
                pltpu.VMEM((ITERS + 1, GROUPS, NC, 128), F32),
                pltpu.VMEM((GROUPS, NC, 128), F32),
                pltpu.VMEM((2, 2, 8 * NC, 128), F32),
                pltpu.VMEM((2, first, 16, 128), F32),
                pltpu.VMEM((2, second, 16, 128), F32),
                pltpu.VMEM((NRHS, NC, 128), BF16),
                pltpu.VMEM((n_gz, per, NC, 128), BF16),
                pltpu.VMEM((per, NC, LOC * n_gz), F32),
                pltpu.VMEM((NC, LOC), F32),
                pltpu.VMEM((NRHS, NC, LOC), F32),
                dma,
                dma,
                dma,
                dma((SLOTS, 9)),
                dma((n_gz,)),
                dma((n_gz,)),
                dma((ITERS, 2, 4)),
                dma((ITERS, 2, 4)),
                dma((ITERS, 2)),
                dma((ITERS, 2)),
                dma((2, first)),
                dma((2, first)),
                dma((2, second)),
                dma((2, second)),
                dma((n_gz,)),
                dma((n_gz,)),
            ],
            compiler_params=pltpu.CompilerParams(
                collective_id=0, has_side_effects=True, vmem_limit_bytes=60 * 1024 * 1024
            ),
        )(restricted, mass_terms, clover_blocks, hop_links)
        return pl.pallas_call(
            deliver,
            out_shape=(
                jax.ShapeDtypeStruct((per, NC, LOC * n_gz), F32),
                jax.ShapeDtypeStruct((NRHS, NC, LOC), F32),
            ),
            in_specs=[vmem, vmem],
            out_specs=(vmem, vmem),
        )(sol, res)

    return jax.shard_map(
        step,
        mesh=mesh,
        in_specs=(
            P("gz", None, "ta"),
            P(None, ("ta", "gz")),
            P(None, None, ("ta", "gz")),
            P(None, None, None, ("ta", "gz")),
        ),
        out_specs=(P("gz", None, "ta"), P(None, None, ("ta", "gz"))),
        check_vma=False,
    )
```

```python
import functools

import jax
import jax.numpy as jnp
from jax import lax
from jax.experimental import pallas as pl
from jax.experimental.pallas import tpu as pltpu
from jax.sharding import PartitionSpec as P

MESH = pl.DeviceIdType.MESH
NC = 96
NRHS = 16
ITERS = 4
LOC = 128
GROUPS = 16
SLOTS = 6
CHUNK = 8
EARLY = 6
SHIFT = 3.0
F32 = jnp.float32
BF16 = jnp.bfloat16


def lanes(rows=8):
    return lax.broadcasted_iota(jnp.int32, (rows, 128), 1)


def mask_for(dtype, condition):
    if dtype == F32:
        return condition
    return jnp.where(condition, 1.0, 0.0).astype(BF16) > 0.5


def swap_blocks(xs):
    lane = lanes(xs[0].shape[0])
    for b in (1, 2, 4, 8):
        shift = 8 * b
        high = mask_for(xs[0].dtype, (lane & shift) != 0)
        new = list(xs)
        for r in range(16):
            if r & b == 0:
                low_x, high_x = xs[r], xs[r | b]
                new[r] = jnp.where(high, pltpu.roll(high_x, shift, 1), low_x)
                new[r | b] = jnp.where(high, high_x, pltpu.roll(low_x, 128 - shift, 1))
        xs = new
    return xs


def sum_sites(x):
    lane = lanes(x.shape[0])
    for shift in (1, 2, 4):
        other = jnp.where((lane & shift) == 0, pltpu.roll(x, 128 - shift, 1), pltpu.roll(x, shift, 1))
        x = x + other
    return x


def block_diagonal(first, second):
    rows = first.shape[0]
    zeros = jnp.zeros((128, 128), BF16)
    parts = []
    for k in range(rows // 128):
        span = slice(128 * k, 128 * k + 128)
        parts.append(jnp.concatenate([first[span], zeros], axis=1))
        parts.append(jnp.concatenate([zeros, second[span]], axis=1))
    return jnp.concatenate(parts, axis=0)


def kernel(
    n_ta, n_gz,
    restricted, mass_in, clover, hops,
    sol_out, res_out,
    links, matrix, perm, stage_in, field_in, own, halo_t, halo_z, ext, mass_f, basis, near, acc,
    part1, part2, back_out, back_in, rhs, mass, res_buf,
    rhs_sem, mass_sem, res_sem, link_sem, in_send, in_recv, t_send, t_recv, z_send, z_recv, s1_send, s1_recv, s2_send, s2_recv, out_send, out_recv,
):
    ta = lax.axis_index("ta")
    gz = lax.axis_index("gz")
    per = NRHS // n_gz
    ta_up, ta_down = (ta + 1) % n_ta, (ta + n_ta - 1) % n_ta
    gz_up, gz_down = (gz + 1) % n_gz, (gz + n_gz - 1) % n_gz
    ta_low, gz_low = min(4, n_ta), min(2, n_gz)
    ta_high, gz_high = n_ta // ta_low, n_gz // gz_low
    th, tl, gh, gl = ta // ta_low, ta % ta_low, gz // gz_low, gz % gz_low
    place1 = tl * gz_low + gl
    place2 = th * gz_high + gh
    peers1 = [
        (th * ta_low + (tl + a) % ta_low, gh * gz_low + (gl + b) % gz_low)
        for a in range(ta_low) for b in range(gz_low) if a or b
    ]
    peers2 = [
        (((th + a) % ta_high) * ta_low + tl, ((gh + b) % gz_high) * gz_low + gl)
        for a in range(ta_high) for b in range(gz_high) if a or b
    ]

    def link_copies(c, slot):
        rows = pl.ds(c * CHUNK, CHUNK)
        copies = [pltpu.make_async_copy(clover.at[rows], links.at[slot, :, 0], link_sem.at[slot, 0])]
        for d in range(8):
            copies.append(
                pltpu.make_async_copy(hops.at[d, rows], links.at[slot, :, d + 1], link_sem.at[slot, d + 1])
            )
        return copies

    rhs_copy = pltpu.make_async_copy(restricted, rhs, rhs_sem)
    rhs_copy.start()
    mass_copy = pltpu.make_async_copy(mass_in, mass, mass_sem)
    mass_copy.start()
    barrier = pltpu.get_barrier_semaphore()
    greet = peers2 + [(ta, (gz + o) % n_gz) for o in range(1, n_gz)] + [(ta_up, gz), (ta_down, gz)] + peers1
    for to in greet:
        pl.semaphore_signal(barrier, inc=1, device_id=to, device_id_type=MESH)

    rhs_copy.wait()
    for c in range(SLOTS):
        for copy in link_copies(c, c):
            copy.start()
    for b in range(n_gz):
        stage_in[b] = rhs[:, :, 128 * b : 128 * b + 128].astype(BF16)
    pl.semaphore_wait(barrier, len(greet))

    def in_copy(o):
        to = (gz + o) % n_gz
        return pltpu.make_async_remote_copy(
            src_ref=stage_in.at[to],
            dst_ref=field_in.at[pl.ds(gz * per, per)],
            send_sem=in_send.at[o],
            recv_sem=in_recv.at[o],
            device_id=(ta, to),
            device_id_type=MESH,
        )

    for o in range(1, n_gz):
        in_copy(o).start()
    field_in[pl.ds(gz * per, per)] = stage_in[gz]

    rows_i = lax.broadcasted_iota(jnp.int32, (256, 256), 0)
    cols_i = lax.broadcasted_iota(jnp.int32, (256, 256), 1)
    wanted = ((rows_i // 8) % 2) * 128 + (rows_i // 16) * 8 + rows_i % 8
    perm[...] = jnp.where(cols_i == wanted, 1.0, 0.0).astype(BF16)

    def mass_step(c, carry):
        rows = pl.ds(pl.multiple_of(c * 16, 16), 16)
        m = mass[rows, :] - SHIFT
        spread = swap_blocks([m] * 16)
        for g in range(GROUPS):
            mass_f[g, rows, :] = spread[g]
        return carry

    mass_copy.wait()
    lax.fori_loop(0, NC // 16, mass_step, 0, unroll=2)

    def prepare(c, carry):
        slot = c % SLOTS
        for copy in link_copies(c, slot):
            copy.wait()
        pad = jnp.zeros((32, 128), BF16)
        for pair in range(CHUNK // 2):
            sides = []
            for i2 in range(2):
                block = links[slot, 2 * pair + i2]
                front = block[:5].reshape(5 * NC, 128)
                tail = block[5:].reshape(4 * NC, 128)
                sides.append(jnp.concatenate([front, pad, tail], axis=0))
            both = jnp.concatenate(sides, axis=1)
            turned = lax.dot_general(
                perm[...], both, (((1,), (1,)), ((), ())), preferred_element_type=F32
            ).astype(BF16)
            rows = pl.ds(pl.multiple_of((c * (CHUNK // 2) + pair) * 16, 16), 16)
            for g in range(GROUPS):
                for k in range(7):
                    start = k * 256 + (g % 2) * 128
                    matrix[g // 2, rows, start : start + 128] = turned[
                        16 * g : 16 * g + 16, 128 * k : 128 * k + 128
                    ]

        @pl.when(c + SLOTS < NC // CHUNK)
        def _():
            for copy in link_copies(c + SLOTS, slot):
                copy.start()

        return carry

    def t_copy(m, t, z):
        side = 1 - t
        return pltpu.make_async_remote_copy(
            src_ref=own.at[m, t, z], dst_ref=halo_t.at[m, side, z],
            send_sem=t_send.at[m, side, z], recv_sem=t_recv.at[m, side, z],
            device_id=(ta_up if t else ta_down, gz), device_id_type=MESH,
        )

    def z_copy(m, side):
        return pltpu.make_async_remote_copy(
            src_ref=own.at[m, :, 0 if side else 3], dst_ref=halo_z.at[m, side],
            send_sem=z_send.at[m, side], recv_sem=z_recv.at[m, side],
            device_id=(ta, gz_down if side else gz_up), device_id_type=MESH,
        )

    def send_rest(m, z):
        t_copy(m, 1, z).start()

        @pl.when(z == 0)
        def _():
            z_copy(m, 1).start()

        @pl.when(z == 3)
        def _():
            z_copy(m, 0).start()

    def chosen(t, half):
        site = lanes() & 7
        parts = []
        for ib in range(NC // 8):
            total = acc[t, half, pl.ds(ib * 64, 8, stride=8), :]
            for s in range(1, 8):
                total = jnp.where(site == s, acc[t, half, pl.ds(ib * 64 + s, 8, stride=8), :], total)
            parts.append(total)
        return jnp.concatenate(parts, axis=0)

    def z_at(i):
        return lax.rem(3 * i, 4)

    def near_dot(k, mix, t, z):
        lane = lanes(NC)
        low_x = mask_for(BF16, (lane & 4) == 0)
        not_last = mask_for(BF16, (lane & 3) < 3)
        not_first = mask_for(BF16, (lane & 3) > 0)
        pad = jnp.zeros((32, 128), BF16)
        vs, swaps, sides = [], [], []
        for half in range(2):
            g = (t * 4 + z) * 2 + half
            if k < ITERS - 1:
                v = basis[k, g]
            else:
                v = mix[0] * basis[1, g]
                for m in range(1, k):
                    v = v + mix[m] * basis[m + 1, g]
            near[g] = mass_f[g] * v
            v = v.astype(BF16)
            vs.append(v)
            swaps.append(jnp.where(low_x, pltpu.roll(v, 124, 1), pltpu.roll(v, 4, 1)))
        for half in range(2):
            v, here, there = vs[half], swaps[half], swaps[1 - half]
            ext[t + 1, z + 1, half] = v
            pieces = [
                v,
                jnp.where(low_x, here, there),
                jnp.where(low_x, there, here),
                jnp.where(not_last, pltpu.roll(v, 127, 1), pltpu.roll(v, 3, 1)),
                jnp.where(not_first, pltpu.roll(v, 1, 1), pltpu.roll(v, 125, 1)),
                pad,
            ]
            sides.append(jnp.concatenate(pieces, axis=0))
        out = jnp.dot(matrix[t * 4 + z, :, :1024], block_diagonal(*sides), preferred_element_type=F32)
        acc[t, 0] = out[:, :128]
        acc[t, 1] = out[:, 128:]

    def near_take(t, z):
        for half in range(2):
            g = (t * 4 + z) * 2 + half
            near[g] += chosen(t, half)

    def near_products(k, mix, i, carry):
        near_dot(k, mix, 0, z_at(i))
        near_take(1, z_at(i + 3))
        near_dot(k, mix, 1, z_at(i))
        near_take(0, z_at(i))
        return carry

    def far_dot(t, z):
        sides = []
        for half in range(2):
            pieces = [
                ext[t + 1, z + 2, half], ext[t + 1, z, half], ext[t + 2, z + 1, half], ext[t, z + 1, half]
            ]
            sides.append(jnp.concatenate(pieces, axis=0))
        out = jnp.dot(matrix[t * 4 + z, :, 1024:], block_diagonal(*sides), preferred_element_type=F32)
        acc[t, 0] = out[:, :128]
        acc[t, 1] = out[:, 128:]

    def far_take(k, t, z):
        sums = None
        for half in range(2):
            g = (t * 4 + z) * 2 + half
            new = near[g] + chosen(t, half)
            basis[k + 1, g] = new
            if k < ITERS - 1:
                own[k + 1, t, z, half] = new.astype(BF16)
            others = [basis[j, g] for j in range(k + 1)]
            products = [other * new for other in others] + [new * new]
            if k == 0:
                products.append(others[0] * others[0])
            part = [jnp.sum(product.reshape(NC // 8, 8, 128), axis=0) for product in products]
            sums = part if sums is None else [a + b for a, b in zip(sums, part)]
        return sums

    def far_products(k, mix, i, carry):
        z = z_at(i)

        def mixed(ref, *at):
            if k < ITERS - 1:
                return ref[(k, *at)]
            v = mix[0] * ref[(1, *at)].astype(F32)
            for m in range(1, k):
                v = v + mix[m] * ref[(m + 1, *at)].astype(F32)
            return v.astype(BF16)

        for t in range(2):
            t_copy(k, 1 - t, z).wait_recv()
            for half in range(2):
                ext[3 * t, z + 1, half] = mixed(halo_t, t, z, half)

        for edge, side in ((0, 0), (3, 1)):

            @pl.when(z == edge)
            def _():
                z_copy(k, side).wait_recv()
                for t in range(2):
                    for half in range(2):
                        ext[t + 1, 5 * side, half] = mixed(halo_z, side, t, half)

        if k == 2:

            @pl.when(i == 1)
            def _():
                sum_middle(0)

        far_dot(0, z)
        before = far_take(k, 1, z_at(i + 3))
        far_dot(1, z)
        now = far_take(k, 0, z)
        if k < ITERS - 1:
            t_copy(k + 1, 0, z).start()

            @pl.when(i > 0)
            def _():
                send_rest(k + 1, z_at(i + 3))

        return tuple(c + jnp.where(i > 0, b, 0.0) + n for c, b, n in zip(carry, before, now))

    def share(number, stage):
        buf, place, peers, send, recv = (
            (part1, place1, peers1, s1_send, s1_recv), (part2, place2, peers2, s2_send, s2_recv)
        )[stage]
        return [
            pltpu.make_async_remote_copy(
                src_ref=buf.at[number, place], dst_ref=buf.at[number, place],
                send_sem=send.at[number, n], recv_sem=recv.at[number, n],
                device_id=to, device_id_type=MESH,
            )
            for n, to in enumerate(peers)
        ]

    def sum_start(number, value):
        part1[number, place1] = value
        for copy in share(number, 0):
            copy.start()

    def sum_middle(number):
        for copy in share(number, 0):
            copy.wait_recv()
        value = part1[number, 0]
        for n in range(1, ta_low * gz_low):
            value = value + part1[number, n]
        part2[number, place2] = value
        for copy in share(number, 1):
            copy.start()

    def sum_end(number):
        for copy in share(number, 1):
            copy.wait_recv()
        value = part2[number, 0]
        for n in range(1, ta_high * gz_high):
            value = value + part2[number, n]
        return sum_sites(value)

    lax.fori_loop(0, EARLY, prepare, 0)
    for o in range(1, n_gz):
        in_copy(o).wait_recv()

    def arrange(c, carry):
        rows = pl.ds(pl.multiple_of(c * 16, 16), 16)
        xs = swap_blocks([field_in[r, rows, :] for r in range(NRHS)])
        for g in range(GROUPS):
            own[0, g // 8, (g // 2) % 4, g % 2, rows, :] = xs[g]
            basis[0, g, rows, :] = xs[g].astype(F32)
        return carry

    lax.fori_loop(0, NC // 16, arrange, 0, unroll=3)
    for z in range(4):
        t_copy(0, 0, z).start()
        t_copy(0, 1, z).start()
    z_copy(0, 1).start()
    z_copy(0, 0).start()
    lax.fori_loop(EARLY, NC // CHUNK, prepare, 0)

    size = ITERS + 1
    gram = {}

    def unit(m):
        return [1.0 if n == m else None for n in range(size)]

    def add(u, c, w):
        out = []
        for a, b in zip(u, w):
            if b is None:
                out.append(a)
            else:
                out.append(c * b if a is None else a + c * b)
        return out

    def scale(c, w):
        return [None if b is None else c * b for b in w]

    def apply_gram(w):
        out = []
        for m in range(size):
            total = None
            for n in range(size):
                if w[n] is not None and (m, n) in gram:
                    term = w[n] * gram[m, n]
                    total = term if total is None else total + term
            out.append(total)
        return out

    def pair_up(u, gw):
        total = None
        for a, b in zip(u, gw):
            if a is not None and b is not None:
                total = a * b if total is None else total + a * b
        return total

    r, p, x = unit(0), unit(1), [None] * size
    images, searches, image_products = [], [], []
    mix = None

    def iterate(k, r, p, x):
        q = add(p, SHIFT, r)
        gq = apply_gram(q)
        betas = [pair_up(image, gq) for image in images]
        qo, po = q, r
        for beta, image, search in zip(betas, images, searches):
            qo, po = add(qo, -beta, image), add(po, -beta, search)
        gqo = apply_gram(qo)
        inverse = 1.0 / jnp.sqrt(jnp.maximum(pair_up(qo, gqo), 0.0) + 1e-06)
        alpha = pair_up(r, gqo) * inverse
        qo, po = scale(inverse, qo), scale(inverse, po)
        x = add(x, alpha, po)
        if k < ITERS - 1:
            product = [None] + p[:-1] if k == 1 else unit(k + 2)
            bq = add(product, SHIFT, p)
            for beta, earlier in zip(betas, image_products):
                bq = add(bq, -beta, earlier)
            bq = scale(inverse, bq)
            image_products.append(bq)
            p = add(p, -alpha, bq)
        r = add(r, -alpha, qo)
        images.append(qo)
        searches.append(po)
        return r, p, x

    def take_gram(pairs, value):
        for n, (i, j) in enumerate(pairs):
            gram[i, j] = gram[j, i] = value[n : n + 1]

    pairs, rows = [], []
    for k in range(ITERS):
        lax.fori_loop(0, 4, functools.partial(near_products, k, mix), 0)
        near_take(1, z_at(3))
        new_pairs = [(j, k + 1) for j in range(k + 2)] + ([(0, 0)] if k == 0 else [])
        zero = jnp.zeros((8, 128), F32)
        sums = lax.fori_loop(0, 4, functools.partial(far_products, k, mix), (zero,) * len(new_pairs))
        sums = [a + b for a, b in zip(sums, far_take(k, 1, z_at(3)))]
        pairs += new_pairs
        rows += [jnp.sum(v, axis=0, keepdims=True) for v in sums]
        if k % 2:
            sum_start(k // 2, jnp.concatenate(rows + [jnp.zeros((16 - len(rows), 128), F32)], axis=0))
            sent, pairs, rows = pairs, [], []
        if k < ITERS - 1:
            t_copy(k + 1, 1, z_at(3)).start()
        if k == 2:
            take_gram(sent, sum_end(0))
            for n in range(2):
                r, p, x = iterate(n, r, p, x)
            mix = p[1:4]
    sum_middle(1)
    take_gram(sent, sum_end(1))
    for n in range(2, ITERS):
        r, p, x = iterate(n, r, p, x)

    def combine(coefs, g, rows):
        total = None
        for m, c in enumerate(coefs):
            if c is not None:
                term = c * basis[m, g, rows, :]
                total = term if total is None else total + term
        return total

    def finish(c, carry):
        rows = pl.ds(pl.multiple_of(c * 16, 16), 16)
        xs = swap_blocks([combine(x, g, rows).astype(BF16) for g in range(GROUPS)])
        for n in range(NRHS):
            back_out[n, rows, :] = xs[n]
        return carry

    lax.fori_loop(0, NC // 16, finish, 0, unroll=3)

    def out_copy(o):
        to = (gz + o) % n_gz
        return pltpu.make_async_remote_copy(
            src_ref=back_out.at[pl.ds(to * per, per)],
            dst_ref=back_in.at[gz],
            send_sem=out_send.at[o],
            recv_sem=out_recv.at[o],
            device_id=(ta, to),
            device_id_type=MESH,
        )

    for o in range(1, n_gz):
        out_copy(o).start()
    back_in[gz] = back_out[pl.ds(gz * per, per)]

    def last_residual(c, carry):
        rows = pl.ds(pl.multiple_of(c * 16, 16), 16)
        xs = swap_blocks([combine(r, g, rows) for g in range(GROUPS)])
        for n in range(NRHS):
            res_buf[n, rows, :] = xs[n]
        return carry

    lax.fori_loop(0, NC // 16, last_residual, 0, unroll=2)
    res_copy = pltpu.make_async_copy(res_buf, res_out, res_sem)
    res_copy.start()

    for o in range(1, n_gz):
        in_copy(o).wait_send()
    for m in range(ITERS):
        for z in range(4):
            t_copy(m, 0, z).wait_send()
            t_copy(m, 1, z).wait_send()
        z_copy(m, 0).wait_send()
        z_copy(m, 1).wait_send()
    for number in range(2):
        for stage in range(2):
            for copy in share(number, stage):
                copy.wait_send()
    for o in range(1, n_gz):
        out_copy(o).wait()
    for b in range(n_gz):
        sol_out[:, :, 128 * b : 128 * b + 128] = back_in[b]
    res_copy.wait()


PIECES = 3


def deliver(sol, res, sol_out, res_out, narrow, wide, held, in_sem, out_sem):
    def piece(n, size):
        return pl.ds(n * (size // PIECES), size // PIECES)

    a = [piece(n, NC) for n in range(PIECES)]
    b = [pl.ds(*at) for at in ((0, 6), (6, 6), (12, 4))]
    fetch, store = [], []
    for n in range(PIECES):
        fetch.append(pltpu.make_async_copy(sol.at[:, a[n]], narrow.at[n], in_sem.at[0, n]))
        fetch.append(pltpu.make_async_copy(res.at[b[n]], held.at[b[n]], in_sem.at[1, n]))
        store.append(pltpu.make_async_copy(wide.at[n], sol_out.at[:, a[n]], out_sem.at[0, n]))
        store.append(pltpu.make_async_copy(held.at[b[n]], res_out.at[b[n]], out_sem.at[1, n]))
    for copy in fetch:
        copy.start()
    for n in range(PIECES):
        fetch[2 * n].wait()
        wide[n] = narrow[n].astype(F32)
        store[2 * n].start()
        fetch[2 * n + 1].wait()
        store[2 * n + 1].start()
    for copy in store:
        copy.wait()


def solution(mesh):
    n_ta, n_gz = mesh.shape["ta"], mesh.shape["gz"]
    per = NRHS // n_gz
    first = min(4, n_ta) * min(2, n_gz)
    second = n_ta * n_gz // first

    def step(restricted, mass_terms, clover_blocks, hop_links):
        vmem = pl.BlockSpec(memory_space=pltpu.VMEM)
        hbm = pl.BlockSpec(memory_space=pl.ANY)
        dma = pltpu.SemaphoreType.DMA
        sol, res = pl.pallas_call(
            functools.partial(kernel, n_ta, n_gz),
            out_shape=(
                jax.ShapeDtypeStruct((per, NC, LOC * n_gz), BF16),
                jax.ShapeDtypeStruct((NRHS, NC, LOC), F32),
            ),
            in_specs=[hbm] * 4,
            out_specs=(vmem, hbm),
            scratch_shapes=[
                pltpu.VMEM((SLOTS, CHUNK, 9, NC, 128), BF16),
                pltpu.VMEM((8, 8 * NC, 7 * 256), BF16),
                pltpu.VMEM((256, 256), BF16),
                pltpu.VMEM((n_gz, per, NC, 128), BF16),
                pltpu.VMEM((NRHS, NC, 128), BF16),
                pltpu.VMEM((ITERS, 2, 4, 2, NC, 128), BF16),
                pltpu.VMEM((ITERS, 2, 4, 2, NC, 128), BF16),
                pltpu.VMEM((ITERS, 2, 2, 2, NC, 128), BF16),
                pltpu.VMEM((4, 6, 2, NC, 128), BF16),
                pltpu.VMEM((GROUPS, NC, 128), F32),
                pltpu.VMEM((ITERS + 1, GROUPS, NC, 128), F32),
                pltpu.VMEM((GROUPS, NC, 128), F32),
                pltpu.VMEM((2, 2, 8 * NC, 128), F32),
                pltpu.VMEM((2, first, 16, 128), F32),
                pltpu.VMEM((2, second, 16, 128), F32),
                pltpu.VMEM((NRHS, NC, 128), BF16),
                pltpu.VMEM((n_gz, per, NC, 128), BF16),
                pltpu.VMEM((per, NC, LOC * n_gz), F32),
                pltpu.VMEM((NC, LOC), F32),
                pltpu.VMEM((NRHS, NC, LOC), F32),
                dma,
                dma,
                dma,
                dma((SLOTS, 9)),
                dma((n_gz,)),
                dma((n_gz,)),
                dma((ITERS, 2, 4)),
                dma((ITERS, 2, 4)),
                dma((ITERS, 2)),
                dma((ITERS, 2)),
                dma((2, first)),
                dma((2, first)),
                dma((2, second)),
                dma((2, second)),
                dma((n_gz,)),
                dma((n_gz,)),
            ],
            compiler_params=pltpu.CompilerParams(
                collective_id=0, has_side_effects=True, vmem_limit_bytes=60 * 1024 * 1024
            ),
        )(restricted, mass_terms, clover_blocks, hop_links)
        return pl.pallas_call(
            deliver,
            out_shape=(
                jax.ShapeDtypeStruct((per, NC, LOC * n_gz), F32),
                jax.ShapeDtypeStruct((NRHS, NC, LOC), F32),
            ),
            in_specs=[hbm, hbm],
            out_specs=(hbm, hbm),
            scratch_shapes=[
                pltpu.VMEM((PIECES, per, NC // PIECES, LOC * n_gz), BF16),
                pltpu.VMEM((PIECES, per, NC // PIECES, LOC * n_gz), F32),
                pltpu.VMEM((NRHS, NC, LOC), F32),
                dma((2, PIECES)),
                dma((2, PIECES)),
            ],
        )(sol, res)

    return jax.shard_map(
        step,
        mesh=mesh,
        in_specs=(
            P("gz", None, "ta"),
            P(None, ("ta", "gz")),
            P(None, None, ("ta", "gz")),
            P(None, None, None, ("ta", "gz")),
        ),
        out_specs=(P("gz", None, "ta"), P(None, None, ("ta", "gz"))),
        check_vma=False,
    )
```

```python
import functools

import jax
import jax.numpy as jnp
from jax import lax
from jax.experimental import pallas as pl
from jax.experimental.pallas import tpu as pltpu
from jax.sharding import PartitionSpec as P

MESH = pl.DeviceIdType.MESH
NC = 96
NRHS = 16
ITERS = 4
LOC = 128
GROUPS = 16
SLOTS = 6
CHUNK = 8
EARLY = 6
SHIFT = 3.0
F32 = jnp.float32
BF16 = jnp.bfloat16


def lanes(rows=8):
    return lax.broadcasted_iota(jnp.int32, (rows, 128), 1)


def mask_for(dtype, condition):
    if dtype == F32:
        return condition
    return jnp.where(condition, 1.0, 0.0).astype(BF16) > 0.5


def swap_blocks(xs):
    lane = lanes(xs[0].shape[0])
    for b in (1, 2, 4, 8):
        shift = 8 * b
        high = mask_for(xs[0].dtype, (lane & shift) != 0)
        new = list(xs)
        for r in range(16):
            if r & b == 0:
                low_x, high_x = xs[r], xs[r | b]
                new[r] = jnp.where(high, pltpu.roll(high_x, shift, 1), low_x)
                new[r | b] = jnp.where(high, high_x, pltpu.roll(low_x, 128 - shift, 1))
        xs = new
    return xs


def sum_sites(x):
    lane = lanes(x.shape[0])
    for shift in (1, 2, 4):
        other = jnp.where((lane & shift) == 0, pltpu.roll(x, 128 - shift, 1), pltpu.roll(x, shift, 1))
        x = x + other
    return x


def block_diagonal(first, second):
    rows = first.shape[0]
    zeros = jnp.zeros((128, 128), BF16)
    parts = []
    for k in range(rows // 128):
        span = slice(128 * k, 128 * k + 128)
        parts.append(jnp.concatenate([first[span], zeros], axis=1))
        parts.append(jnp.concatenate([zeros, second[span]], axis=1))
    return jnp.concatenate(parts, axis=0)


def kernel(
    n_ta, n_gz,
    restricted, mass_in, clover, hops,
    sol_out, res_out,
    links, matrix, perm, stage_in, field_in, own, halo_t, halo_z, ext, mass_f, basis, near, acc,
    part1, part2, back_out, back_in, rhs, mass, res_buf,
    rhs_sem, mass_sem, res_sem, link_sem, in_send, in_recv, t_send, t_recv, z_send, z_recv, s1_send, s1_recv, s2_send, s2_recv, out_send, out_recv,
):
    ta = lax.axis_index("ta")
    gz = lax.axis_index("gz")
    per = NRHS // n_gz
    ta_up, ta_down = (ta + 1) % n_ta, (ta + n_ta - 1) % n_ta
    gz_up, gz_down = (gz + 1) % n_gz, (gz + n_gz - 1) % n_gz
    ta_low, gz_low = min(4, n_ta), min(2, n_gz)
    ta_high, gz_high = n_ta // ta_low, n_gz // gz_low
    th, tl, gh, gl = ta // ta_low, ta % ta_low, gz // gz_low, gz % gz_low
    place1 = tl * gz_low + gl
    place2 = th * gz_high + gh
    peers1 = [
        (th * ta_low + (tl + a) % ta_low, gh * gz_low + (gl + b) % gz_low)
        for a in range(ta_low) for b in range(gz_low) if a or b
    ]
    peers2 = [
        (((th + a) % ta_high) * ta_low + tl, ((gh + b) % gz_high) * gz_low + gl)
        for a in range(ta_high) for b in range(gz_high) if a or b
    ]

    def link_copies(c, slot):
        rows = pl.ds(c * CHUNK, CHUNK)
        copies = [pltpu.make_async_copy(clover.at[rows], links.at[slot, :, 0], link_sem.at[slot, 0])]
        for d in range(8):
            copies.append(
                pltpu.make_async_copy(hops.at[d, rows], links.at[slot, :, d + 1], link_sem.at[slot, d + 1])
            )
        return copies

    rhs_copy = pltpu.make_async_copy(restricted, rhs, rhs_sem)
    rhs_copy.start()
    mass_copy = pltpu.make_async_copy(mass_in, mass, mass_sem)
    mass_copy.start()
    barrier = pltpu.get_barrier_semaphore()
    greet = peers2 + [(ta, (gz + o) % n_gz) for o in range(1, n_gz)] + [(ta_up, gz), (ta_down, gz)] + peers1
    for to in greet:
        pl.semaphore_signal(barrier, inc=1, device_id=to, device_id_type=MESH)

    rhs_copy.wait()
    for c in range(SLOTS):
        for copy in link_copies(c, c):
            copy.start()
    for b in range(n_gz):
        stage_in[b] = rhs[:, :, 128 * b : 128 * b + 128].astype(BF16)
    pl.semaphore_wait(barrier, len(greet))

    def in_copy(o):
        to = (gz + o) % n_gz
        return pltpu.make_async_remote_copy(
            src_ref=stage_in.at[to],
            dst_ref=field_in.at[pl.ds(gz * per, per)],
            send_sem=in_send.at[o],
            recv_sem=in_recv.at[o],
            device_id=(ta, to),
            device_id_type=MESH,
        )

    for o in range(1, n_gz):
        in_copy(o).start()
    field_in[pl.ds(gz * per, per)] = stage_in[gz]

    rows_i = lax.broadcasted_iota(jnp.int32, (256, 256), 0)
    cols_i = lax.broadcasted_iota(jnp.int32, (256, 256), 1)
    wanted = ((rows_i // 8) % 2) * 128 + (rows_i // 16) * 8 + rows_i % 8
    perm[...] = jnp.where(cols_i == wanted, 1.0, 0.0).astype(BF16)

    def mass_step(c, carry):
        rows = pl.ds(pl.multiple_of(c * 16, 16), 16)
        m = mass[rows, :] - SHIFT
        spread = swap_blocks([m] * 16)
        for g in range(GROUPS):
            mass_f[g, rows, :] = spread[g]
        return carry

    mass_copy.wait()
    lax.fori_loop(0, NC // 16, mass_step, 0, unroll=2)

    def prepare(c, carry):
        slot = c % SLOTS
        for copy in link_copies(c, slot):
            copy.wait()
        pad = jnp.zeros((32, 128), BF16)
        for pair in range(CHUNK // 2):
            sides = []
            for i2 in range(2):
                block = links[slot, 2 * pair + i2]
                front = block[:5].reshape(5 * NC, 128)
                tail = block[5:].reshape(4 * NC, 128)
                sides.append(jnp.concatenate([front, pad, tail], axis=0))
            both = jnp.concatenate(sides, axis=1)
            turned = lax.dot_general(
                perm[...], both, (((1,), (1,)), ((), ())), preferred_element_type=F32
            ).astype(BF16)
            rows = pl.ds(pl.multiple_of((c * (CHUNK // 2) + pair) * 16, 16), 16)
            for g in range(GROUPS):
                for k in range(7):
                    start = k * 256 + (g % 2) * 128
                    matrix[g // 2, rows, start : start + 128] = turned[
                        16 * g : 16 * g + 16, 128 * k : 128 * k + 128
                    ]

        @pl.when(c + SLOTS < NC // CHUNK)
        def _():
            for copy in link_copies(c + SLOTS, slot):
                copy.start()

        return carry

    def t_copy(m, t, z):
        side = 1 - t
        return pltpu.make_async_remote_copy(
            src_ref=own.at[m, t, z], dst_ref=halo_t.at[m, side, z],
            send_sem=t_send.at[m, side, z], recv_sem=t_recv.at[m, side, z],
            device_id=(ta_up if t else ta_down, gz), device_id_type=MESH,
        )

    def z_copy(m, side):
        return pltpu.make_async_remote_copy(
            src_ref=own.at[m, :, 0 if side else 3], dst_ref=halo_z.at[m, side],
            send_sem=z_send.at[m, side], recv_sem=z_recv.at[m, side],
            device_id=(ta, gz_down if side else gz_up), device_id_type=MESH,
        )

    def send_rest(m, z):
        t_copy(m, 1, z).start()

        @pl.when(z == 0)
        def _():
            z_copy(m, 1).start()

        @pl.when(z == 3)
        def _():
            z_copy(m, 0).start()

    def chosen(t, half):
        site = lanes() & 7
        parts = []
        for ib in range(NC // 8):
            total = acc[t, half, pl.ds(ib * 64, 8, stride=8), :]
            for s in range(1, 8):
                total = jnp.where(site == s, acc[t, half, pl.ds(ib * 64 + s, 8, stride=8), :], total)
            parts.append(total)
        return jnp.concatenate(parts, axis=0)

    def z_at(i):
        return lax.rem(3 * i, 4)

    def near_dot(k, mix, t, z):
        lane = lanes(NC)
        low_x = mask_for(BF16, (lane & 4) == 0)
        not_last = mask_for(BF16, (lane & 3) < 3)
        not_first = mask_for(BF16, (lane & 3) > 0)
        pad = jnp.zeros((32, 128), BF16)
        vs, swaps, sides = [], [], []
        for half in range(2):
            g = (t * 4 + z) * 2 + half
            if k < ITERS - 1:
                v = basis[k, g]
            else:
                v = mix[0] * basis[1, g]
                for m in range(1, k):
                    v = v + mix[m] * basis[m + 1, g]
            near[g] = mass_f[g] * v
            v = v.astype(BF16)
            vs.append(v)
            swaps.append(jnp.where(low_x, pltpu.roll(v, 124, 1), pltpu.roll(v, 4, 1)))
        for half in range(2):
            v, here, there = vs[half], swaps[half], swaps[1 - half]
            ext[t + 1, z + 1, half] = v
            pieces = [
                v,
                jnp.where(low_x, here, there),
                jnp.where(low_x, there, here),
                jnp.where(not_last, pltpu.roll(v, 127, 1), pltpu.roll(v, 3, 1)),
                jnp.where(not_first, pltpu.roll(v, 1, 1), pltpu.roll(v, 125, 1)),
                pad,
            ]
            sides.append(jnp.concatenate(pieces, axis=0))
        out = jnp.dot(matrix[t * 4 + z, :, :1024], block_diagonal(*sides), preferred_element_type=F32)
        acc[t, 0] = out[:, :128]
        acc[t, 1] = out[:, 128:]

    def near_take(t, z):
        for half in range(2):
            g = (t * 4 + z) * 2 + half
            near[g] += chosen(t, half)

    def near_products(k, mix, i, carry):
        near_dot(k, mix, 0, z_at(i))
        near_take(1, z_at(i + 3))
        near_dot(k, mix, 1, z_at(i))
        near_take(0, z_at(i))
        return carry

    def far_dot(t, z):
        sides = []
        for half in range(2):
            pieces = [
                ext[t + 1, z + 2, half], ext[t + 1, z, half], ext[t + 2, z + 1, half], ext[t, z + 1, half]
            ]
            sides.append(jnp.concatenate(pieces, axis=0))
        out = jnp.dot(matrix[t * 4 + z, :, 1024:], block_diagonal(*sides), preferred_element_type=F32)
        acc[t, 0] = out[:, :128]
        acc[t, 1] = out[:, 128:]

    def far_take(k, t, z):
        sums = None
        for half in range(2):
            g = (t * 4 + z) * 2 + half
            new = near[g] + chosen(t, half)
            basis[k + 1, g] = new
            if k < ITERS - 1:
                own[k + 1, t, z, half] = new.astype(BF16)
            others = [basis[j, g] for j in range(k + 1)]
            products = [other * new for other in others] + [new * new]
            if k == 0:
                products.append(others[0] * others[0])
            part = [jnp.sum(product.reshape(NC // 8, 8, 128), axis=0) for product in products]
            sums = part if sums is None else [a + b for a, b in zip(sums, part)]
        return sums

    def far_products(k, mix, i, carry):
        z = z_at(i)

        def mixed(ref, *at):
            if k < ITERS - 1:
                return ref[(k, *at)]
            v = mix[0] * ref[(1, *at)].astype(F32)
            for m in range(1, k):
                v = v + mix[m] * ref[(m + 1, *at)].astype(F32)
            return v.astype(BF16)

        for t in range(2):
            t_copy(k, 1 - t, z).wait_recv()
            for half in range(2):
                ext[3 * t, z + 1, half] = mixed(halo_t, t, z, half)

        for edge, side in ((0, 0), (3, 1)):

            @pl.when(z == edge)
            def _():
                z_copy(k, side).wait_recv()
                for t in range(2):
                    for half in range(2):
                        ext[t + 1, 5 * side, half] = mixed(halo_z, side, t, half)

        if k == 2:

            @pl.when(i == 1)
            def _():
                sum_middle(0)

        far_dot(0, z)
        before = far_take(k, 1, z_at(i + 3))
        far_dot(1, z)
        now = far_take(k, 0, z)
        if k < ITERS - 1:
            t_copy(k + 1, 0, z).start()

            @pl.when(i > 0)
            def _():
                send_rest(k + 1, z_at(i + 3))

        return tuple(c + jnp.where(i > 0, b, 0.0) + n for c, b, n in zip(carry, before, now))

    def share(number, stage):
        buf, place, peers, send, recv = (
            (part1, place1, peers1, s1_send, s1_recv), (part2, place2, peers2, s2_send, s2_recv)
        )[stage]
        return [
            pltpu.make_async_remote_copy(
                src_ref=buf.at[number, place], dst_ref=buf.at[number, place],
                send_sem=send.at[number, n], recv_sem=recv.at[number, n],
                device_id=to, device_id_type=MESH,
            )
            for n, to in enumerate(peers)
        ]

    def sum_start(number, value):
        part1[number, place1] = value
        for copy in share(number, 0):
            copy.start()

    def sum_middle(number):
        for copy in share(number, 0):
            copy.wait_recv()
        value = part1[number, 0]
        for n in range(1, ta_low * gz_low):
            value = value + part1[number, n]
        part2[number, place2] = value
        for copy in share(number, 1):
            copy.start()

    def sum_end(number):
        for copy in share(number, 1):
            copy.wait_recv()
        value = part2[number, 0]
        for n in range(1, ta_high * gz_high):
            value = value + part2[number, n]
        return sum_sites(value)

    lax.fori_loop(0, EARLY, prepare, 0)
    for o in range(1, n_gz):
        in_copy(o).wait_recv()

    def arrange(c, carry):
        rows = pl.ds(pl.multiple_of(c * 16, 16), 16)
        xs = swap_blocks([field_in[r, rows, :] for r in range(NRHS)])
        for g in range(GROUPS):
            own[0, g // 8, (g // 2) % 4, g % 2, rows, :] = xs[g]
            basis[0, g, rows, :] = xs[g].astype(F32)
        return carry

    lax.fori_loop(0, NC // 16, arrange, 0, unroll=3)
    for z in range(4):
        t_copy(0, 0, z).start()
        t_copy(0, 1, z).start()
    z_copy(0, 1).start()
    z_copy(0, 0).start()
    lax.fori_loop(EARLY, NC // CHUNK, prepare, 0)

    size = ITERS + 1
    gram = {}

    def unit(m):
        return [1.0 if n == m else None for n in range(size)]

    def add(u, c, w):
        out = []
        for a, b in zip(u, w):
            if b is None:
                out.append(a)
            else:
                out.append(c * b if a is None else a + c * b)
        return out

    def scale(c, w):
        return [None if b is None else c * b for b in w]

    def apply_gram(w):
        out = []
        for m in range(size):
            total = None
            for n in range(size):
                if w[n] is not None and (m, n) in gram:
                    term = w[n] * gram[m, n]
                    total = term if total is None else total + term
            out.append(total)
        return out

    def pair_up(u, gw):
        total = None
        for a, b in zip(u, gw):
            if a is not None and b is not None:
                total = a * b if total is None else total + a * b
        return total

    r, p, x = unit(0), unit(1), [None] * size
    images, searches, image_products = [], [], []
    mix = None

    def iterate(k, r, p, x):
        q = add(p, SHIFT, r)
        gq = apply_gram(q)
        betas = [pair_up(image, gq) for image in images]
        qo, po = q, r
        for beta, image, search in zip(betas, images, searches):
            qo, po = add(qo, -beta, image), add(po, -beta, search)
        gqo = apply_gram(qo)
        inverse = 1.0 / jnp.sqrt(jnp.maximum(pair_up(qo, gqo), 0.0) + 1e-06)
        alpha = pair_up(r, gqo) * inverse
        qo, po = scale(inverse, qo), scale(inverse, po)
        x = add(x, alpha, po)
        if k < ITERS - 1:
            product = [None] + p[:-1] if k == 1 else unit(k + 2)
            bq = add(product, SHIFT, p)
            for beta, earlier in zip(betas, image_products):
                bq = add(bq, -beta, earlier)
            bq = scale(inverse, bq)
            image_products.append(bq)
            p = add(p, -alpha, bq)
        r = add(r, -alpha, qo)
        images.append(qo)
        searches.append(po)
        return r, p, x

    def out_copy(m, o):
        to = (gz + o) % n_gz
        return pltpu.make_async_remote_copy(
            src_ref=back_out.at[m - 1, pl.ds(to * per, per)],
            dst_ref=back_in.at[m - 1, gz],
            send_sem=out_send.at[m - 1, o],
            recv_sem=out_recv.at[m - 1, o],
            device_id=(ta, to),
            device_id_type=MESH,
        )

    def send_back(m):
        def turn(c, carry):
            rows = pl.ds(pl.multiple_of(c * 16, 16), 16)
            xs = swap_blocks([own[m, g // 8, (g // 2) % 4, g % 2, rows, :] for g in range(GROUPS)])
            for n in range(NRHS):
                back_out[m - 1, n, rows, :] = xs[n]
            return carry

        lax.fori_loop(0, NC // 16, turn, 0, unroll=3)
        for o in range(1, n_gz):
            out_copy(m, o).start()
        back_in[m - 1, gz] = back_out[m - 1, pl.ds(gz * per, per)]

    def take_gram(pairs, value):
        for n, (i, j) in enumerate(pairs):
            gram[i, j] = gram[j, i] = value[n : n + 1]

    pairs, rows = [], []
    for k in range(ITERS):
        lax.fori_loop(0, 4, functools.partial(near_products, k, mix), 0)
        near_take(1, z_at(3))
        new_pairs = [(j, k + 1) for j in range(k + 2)] + ([(0, 0)] if k == 0 else [])
        zero = jnp.zeros((8, 128), F32)
        sums = lax.fori_loop(0, 4, functools.partial(far_products, k, mix), (zero,) * len(new_pairs))
        sums = [a + b for a, b in zip(sums, far_take(k, 1, z_at(3)))]
        pairs += new_pairs
        rows += [jnp.sum(v, axis=0, keepdims=True) for v in sums]
        if k % 2:
            sum_start(k // 2, jnp.concatenate(rows + [jnp.zeros((16 - len(rows), 128), F32)], axis=0))
            sent, pairs, rows = pairs, [], []
        if k < ITERS - 1:
            t_copy(k + 1, 1, z_at(3)).start()
        if k == 2:
            take_gram(sent, sum_end(0))
            for n in range(2):
                r, p, x = iterate(n, r, p, x)
            mix = p[1:4]
            for m in range(1, ITERS):
                send_back(m)
    sum_middle(1)
    take_gram(sent, sum_end(1))
    for n in range(2, ITERS):
        r, p, x = iterate(n, r, p, x)

    def combine(coefs, g, rows):
        total = None
        for m, c in enumerate(coefs):
            if c is not None:
                term = c * basis[m, g, rows, :]
                total = term if total is None else total + term
        return total

    def last_residual(c, carry):
        rows = pl.ds(pl.multiple_of(c * 16, 16), 16)
        xs = swap_blocks([combine(r, g, rows) for g in range(GROUPS)])
        for n in range(NRHS):
            res_buf[n, rows, :] = xs[n]
        return carry

    lax.fori_loop(0, NC // 16, last_residual, 0, unroll=2)
    res_copy = pltpu.make_async_copy(res_buf, res_out, res_sem)
    res_copy.start()

    for o in range(1, n_gz):
        in_copy(o).wait_send()
    for m in range(ITERS):
        for z in range(4):
            t_copy(m, 0, z).wait_send()
            t_copy(m, 1, z).wait_send()
        z_copy(m, 0).wait_send()
        z_copy(m, 1).wait_send()
    for number in range(2):
        for stage in range(2):
            for copy in share(number, stage):
                copy.wait_send()
    for m in range(1, ITERS):
        for o in range(1, n_gz):
            out_copy(m, o).wait()
    for n in range(per):
        mine = lanes(1) == 8 * (gz * per + n)
        parts = [jnp.sum(jnp.where(mine, x[m], 0.0), axis=1, keepdims=True) for m in range(ITERS)]
        for b in range(n_gz):
            total = parts[0] * stage_in[b, n].astype(F32)
            for m in range(1, ITERS):
                total = total + parts[m] * back_in[m - 1, b, n].astype(F32)
            sol_out[n, :, 128 * b : 128 * b + 128] = total.astype(BF16)
    res_copy.wait()


PIECES = 3


def deliver(sol, res, sol_out, res_out, narrow, wide, held, in_sem, out_sem):
    def piece(n, size):
        return pl.ds(n * (size // PIECES), size // PIECES)

    a = [piece(n, NC) for n in range(PIECES)]
    b = [pl.ds(*at) for at in ((0, 6), (6, 6), (12, 4))]
    fetch, store = [], []
    for n in range(PIECES):
        fetch.append(pltpu.make_async_copy(sol.at[:, a[n]], narrow.at[n], in_sem.at[0, n]))
        fetch.append(pltpu.make_async_copy(res.at[b[n]], held.at[b[n]], in_sem.at[1, n]))
        store.append(pltpu.make_async_copy(wide.at[n], sol_out.at[:, a[n]], out_sem.at[0, n]))
        store.append(pltpu.make_async_copy(held.at[b[n]], res_out.at[b[n]], out_sem.at[1, n]))
    for copy in fetch:
        copy.start()
    for n in range(PIECES):
        fetch[2 * n].wait()
        wide[n] = narrow[n].astype(F32)
        store[2 * n].start()
        fetch[2 * n + 1].wait()
        store[2 * n + 1].start()
    for copy in store:
        copy.wait()


def solution(mesh):
    n_ta, n_gz = mesh.shape["ta"], mesh.shape["gz"]
    per = NRHS // n_gz
    first = min(4, n_ta) * min(2, n_gz)
    second = n_ta * n_gz // first

    def step(restricted, mass_terms, clover_blocks, hop_links):
        vmem = pl.BlockSpec(memory_space=pltpu.VMEM)
        hbm = pl.BlockSpec(memory_space=pl.ANY)
        dma = pltpu.SemaphoreType.DMA
        sol, res = pl.pallas_call(
            functools.partial(kernel, n_ta, n_gz),
            out_shape=(
                jax.ShapeDtypeStruct((per, NC, LOC * n_gz), BF16),
                jax.ShapeDtypeStruct((NRHS, NC, LOC), F32),
            ),
            in_specs=[hbm] * 4,
            out_specs=(vmem, hbm),
            scratch_shapes=[
                pltpu.VMEM((SLOTS, CHUNK, 9, NC, 128), BF16),
                pltpu.VMEM((8, 8 * NC, 7 * 256), BF16),
                pltpu.VMEM((256, 256), BF16),
                pltpu.VMEM((n_gz, per, NC, 128), BF16),
                pltpu.VMEM((NRHS, NC, 128), BF16),
                pltpu.VMEM((ITERS, 2, 4, 2, NC, 128), BF16),
                pltpu.VMEM((ITERS, 2, 4, 2, NC, 128), BF16),
                pltpu.VMEM((ITERS, 2, 2, 2, NC, 128), BF16),
                pltpu.VMEM((4, 6, 2, NC, 128), BF16),
                pltpu.VMEM((GROUPS, NC, 128), F32),
                pltpu.VMEM((ITERS + 1, GROUPS, NC, 128), F32),
                pltpu.VMEM((GROUPS, NC, 128), F32),
                pltpu.VMEM((2, 2, 8 * NC, 128), F32),
                pltpu.VMEM((2, first, 16, 128), F32),
                pltpu.VMEM((2, second, 16, 128), F32),
                pltpu.VMEM((ITERS - 1, NRHS, NC, 128), BF16),
                pltpu.VMEM((ITERS - 1, n_gz, per, NC, 128), BF16),
                pltpu.VMEM((per, NC, LOC * n_gz), F32),
                pltpu.VMEM((NC, LOC), F32),
                pltpu.VMEM((NRHS, NC, LOC), F32),
                dma,
                dma,
                dma,
                dma((SLOTS, 9)),
                dma((n_gz,)),
                dma((n_gz,)),
                dma((ITERS, 2, 4)),
                dma((ITERS, 2, 4)),
                dma((ITERS, 2)),
                dma((ITERS, 2)),
                dma((2, first)),
                dma((2, first)),
                dma((2, second)),
                dma((2, second)),
                dma((ITERS - 1, n_gz)),
                dma((ITERS - 1, n_gz)),
            ],
            compiler_params=pltpu.CompilerParams(
                collective_id=0, has_side_effects=True, vmem_limit_bytes=60 * 1024 * 1024
            ),
        )(restricted, mass_terms, clover_blocks, hop_links)
        return pl.pallas_call(
            deliver,
            out_shape=(
                jax.ShapeDtypeStruct((per, NC, LOC * n_gz), F32),
                jax.ShapeDtypeStruct((NRHS, NC, LOC), F32),
            ),
            in_specs=[hbm, hbm],
            out_specs=(hbm, hbm),
            scratch_shapes=[
                pltpu.VMEM((PIECES, per, NC // PIECES, LOC * n_gz), BF16),
                pltpu.VMEM((PIECES, per, NC // PIECES, LOC * n_gz), F32),
                pltpu.VMEM((NRHS, NC, LOC), F32),
                dma((2, PIECES)),
                dma((2, PIECES)),
            ],
        )(sol, res)

    return jax.shard_map(
        step,
        mesh=mesh,
        in_specs=(
            P("gz", None, "ta"),
            P(None, ("ta", "gz")),
            P(None, None, ("ta", "gz")),
            P(None, None, None, ("ta", "gz")),
        ),
        out_specs=(P("gz", None, "ta"), P(None, None, ("ta", "gz"))),
        check_vma=False,
    )
```
